32 devices in a mesh: groups: 2 (over y), owner: 8 (over z, x), batch: 2 (over core).
Axes of the slice: x: 2, y: 2, z: 4, core: 2. Of those that a mesh axis runs over, the one named last changes fastest.
Arguments:
- features: bfloat16 [4096, 768], P('owner'), may hold values from -12 to 12
- w_first: bfloat16 [768, 512], replicated, may hold values from -0.21875 to 0.21875
- w_second: bfloat16 [512, 512], replicated, may hold values from -0.25 to 0.25
- w_third: bfloat16 [512, 153], replicated, may hold values from -0.25 to 0.25
- nbr_ids: int32 [512, 32], P(('groups', 'owner', 'batch')), parts along dimension 0, may hold values from 0 to 4095, as said below
- nbr_weight: float32 [512, 32], P(('groups', 'owner', 'batch')), parts along dimension 0, may hold values from 0.05 to 0.5
- labels: int32 [512], P(('groups', 'owner', 'batch')), parts along dimension 0, may hold values from 0 to 152
Outputs:
- grad_first: bfloat16 [1536, 512], P('groups'), parts along dimension 0
- grad_second: bfloat16 [1024, 512], P('groups'), parts along dimension 0
- grad_third: bfloat16 [1024, 153], P('groups'), parts along dimension 0
- target_loss: float32 [512], P(('groups', 'owner', 'batch')), parts along dimension 0
The draws below stay inside these ranges and needn't reach their ends.
There are 2 independent parts, one for each index of `groups`. The reference program is written for one: setup_inputs(seed, part) draws one part's arguments, and reference() takes and returns one part's arrays. A program takes and returns all parts, laid end to end along the dimension named above; an argument that names none is the same for every part. Nothing has to cross between parts.
Inputs may be any that keep to these rules, and one draw needn't show every extreme that they name: `nbr_ids`: node n belongs to owner n // 512. In each device's block of 16 targets the 32 neighbour ids of all its targets fall at most 128 times in one owner's nodes, and exactly 128 times for at least one owner.
All inputs are finite; a program needn't handle non-finite values.
Results may differ from the reference program's by a relative error of at most 0.0063.
Values may be sent and summed in bfloat16 or wider, within the bound.
No kernel may reach another device: no remote copies, remote signals or barrier semaphores. Data moves between devices by JAX's collectives and lax.ppermute only.
A program may use at most 64 MiB of HBM per device.

```python
import math
import jax
import jax.numpy as jnp
from jax import lax

D = 768
H = 512
C = 153
K = 32
T_DEV = 16
NODE_DEV = 512
CAP = 128
TARGETS = 256
NODES = 4096
N_OWNER = 8
N_BATCH = 2


def owner_block(key):
    hottest = jax.random.randint(jax.random.fold_in(key, 1), (), 0, N_OWNER)
    order = jax.random.permutation(jax.random.fold_in(key, 2), (N_OWNER - 1) * CAP)[:T_DEV * K - CAP]
    others = (order // CAP).astype(jnp.int32)
    others = others + (others >= hottest).astype(jnp.int32)
    owner_list = jnp.concatenate([jnp.full((CAP,), hottest, jnp.int32), others])
    owner_list = jax.random.permutation(jax.random.fold_in(key, 3), owner_list).astype(jnp.int32)
    local_rows = jax.random.randint(jax.random.fold_in(key, 4), (T_DEV * K,), 0, NODE_DEV).astype(jnp.int32)
    return (owner_list * NODE_DEV + local_rows).reshape(T_DEV, K)


def draw_nbr_ids(key, part):
    key = jax.random.fold_in(key, 7)
    keys = jax.random.split(key, N_OWNER * N_BATCH)
    return jax.vmap(owner_block)(keys).reshape(TARGETS, K).astype(jnp.int32)


def draw_features(key, part):
    key = jax.random.fold_in(key, 13)
    values = jax.random.normal(key, (NODES, D))
    return values.astype(jnp.float32).astype(jnp.bfloat16)


def plant(result, key, least, high):
    longest = result.shape.index(max(result.shape))
    spots = []
    for shift in (0, 1):
        where = [jax.random.randint(jax.random.fold_in(key, axis), (), 0, length) for axis, length in enumerate(result.shape)]
        where[longest] = (where[longest] + shift) % result.shape[longest]
        spots.append(tuple(where))
    return result.at[spots[0]].set(least).at[spots[1]].set(high)


def steps_of(own_key, dims, cuts, smallest, largest):
    def one(axis_at, blocks):
        steps = jax.random.uniform(jax.random.fold_in(jax.random.fold_in(own_key, 6), axis_at), (blocks,), jnp.float32, smallest / len(cuts), largest / len(cuts))
        return jnp.repeat(jnp.exp(steps), dims[axis_at] // blocks).reshape((-1,) + (1,) * (len(dims) - axis_at - 1))

    gain = one(*cuts[0])
    for cut in cuts[1:]:
        gain = gain * one(*cut)
    return gain


def bell_draw(stream_key, extent, width, limit, kind=jnp.bfloat16):
    entries = width * jax.random.normal(stream_key, extent, jnp.float32)
    return jnp.clip(entries, min=-limit, max=limit).astype(kind)


def setup_inputs(seed: int = 0, part: int = 0) -> dict:
    arg_keys = jax.random.split(jax.random.key(seed), 8)
    part_splits = jax.random.split(jax.random.fold_in(arg_keys[7], part), 8)
    features = draw_features(jax.random.fold_in(arg_keys[7], 71), part)
    w_first = bell_draw(arg_keys[1], (D, H), D ** -0.5, 0.21875)
    w_second = bell_draw(arg_keys[2], (H, H), H ** -0.5, 0.25)
    w_third = bell_draw(arg_keys[3], (H, C), H ** -0.5, 0.25)
    nbr_ids = draw_nbr_ids(jax.random.fold_in(jax.random.fold_in(arg_keys[7], part), 71), part)
    nbr_weight = jnp.clip(jnp.exp(math.log(0.5) - 2.3025851 * jax.random.uniform(part_splits[5], (TARGETS, K), jnp.float32) ** steps_of(part_splits[5], (TARGETS, K), ((0, 16),), -0.2, 0.2)), 0.05, 0.5)
    labels = plant(jax.random.randint(part_splits[6], (TARGETS,), 0, C), jax.random.fold_in(part_splits[6], 1), 0, C - 1).astype(jnp.int32)
    return {"features": features, "w_first": w_first, "w_second": w_second, "w_third": w_third, "nbr_ids": nbr_ids, "nbr_weight": nbr_weight, "labels": labels}


def silu_slope(pre):
    sigma = jax.nn.sigmoid(pre)
    return sigma * (1.0 + pre * (1.0 - sigma))


def reference(features, w_first, w_second, w_third, nbr_ids, nbr_weight, labels):
    blocks = TARGETS // T_DEV
    classes = w_third.shape[1]
    ids_blocks = nbr_ids.reshape(blocks, T_DEV, K)
    weight_blocks = nbr_weight.reshape(blocks, T_DEV, K)
    label_blocks = labels.reshape(blocks, T_DEV)

    def advance(totals, block):
        ids_block, weight_block, label_block = block
        inputs = features[ids_block.reshape(-1)]
        pre_one = jnp.dot(inputs, w_first, preferred_element_type=jnp.float32)
        hidden_one = jax.nn.silu(pre_one).astype(jnp.bfloat16)
        pre_two = jnp.dot(hidden_one, w_second, preferred_element_type=jnp.float32)
        hidden_two = jax.nn.silu(pre_two).astype(jnp.bfloat16)
        scores = jnp.dot(hidden_two, w_third, preferred_element_type=jnp.float32).astype(jnp.bfloat16)
        scores = lax.optimization_barrier(scores)
        logits = jnp.sum(weight_block[:, :, None] * scores.reshape(T_DEV, K, classes).astype(jnp.float32), axis=1)
        log_prob = jax.nn.log_softmax(logits)
        target = jax.nn.one_hot(label_block, classes, dtype=jnp.float32)
        losses = -jnp.sum(target * log_prob, axis=1)
        grad_logits = jnp.exp(log_prob) - target
        entry_grads = (weight_block[:, :, None] * grad_logits[:, None, :]).astype(jnp.bfloat16).reshape(T_DEV * K, classes)
        grad_third = jnp.dot(hidden_two.T, entry_grads, preferred_element_type=jnp.float32)
        back_two = (jnp.dot(entry_grads, w_third.T, preferred_element_type=jnp.float32) * silu_slope(pre_two)).astype(jnp.bfloat16)
        grad_second = jnp.dot(hidden_one.T, back_two, preferred_element_type=jnp.float32)
        back_one = (jnp.dot(back_two, w_second.T, preferred_element_type=jnp.float32) * silu_slope(pre_one)).astype(jnp.bfloat16)
        grad_first = jnp.dot(inputs.T, back_one, preferred_element_type=jnp.float32)
        return (totals[0] + grad_first, totals[1] + grad_second, totals[2] + grad_third), losses

    start = (jnp.zeros(w_first.shape, jnp.float32), jnp.zeros(w_second.shape, jnp.float32), jnp.zeros(w_third.shape, jnp.float32))
    totals, losses = lax.scan(advance, start, (ids_blocks, weight_blocks, label_blocks))
    return (totals[0].astype(jnp.bfloat16), totals[1].astype(jnp.bfloat16), totals[2].astype(jnp.bfloat16), losses.reshape(-1))
```

```python
import functools
import jax
import jax.numpy as jnp
from jax import lax
from jax.experimental import pallas as pl
from jax.experimental.pallas import tpu as pltpu
from jax.sharding import PartitionSpec as P

BF = jnp.bfloat16
F32 = jnp.float32
ROW = 16
LANE = 128


def nn(a, b):
    return lax.dot_general(a, b, (((1,), (0,)), ((), ())), preferred_element_type=F32)


def nt(a, b):
    return lax.dot_general(a, b, (((1,), (1,)), ((), ())), preferred_element_type=F32)


def tn(a, b):
    return lax.dot_general(a, b, (((0,), (0,)), ((), ())), preferred_element_type=F32)


def split(v):
    high = v.astype(BF)
    return high, (v - high.astype(F32)).astype(BF)


def device_slice():
    place = lax.rem(lax.axis_index("owner"), 2) * 2 + lax.axis_index("batch")
    return pl.multiple_of(place * LANE, LANE)


def layers(rows, w_first, w_second, h1, h2, s1, s2, one, two):
    pre = nn(rows, w_first)
    sigma = 1.0 / (1.0 + jnp.exp(-pre))
    hidden = (pre * sigma).astype(BF)
    h1[...] = hidden
    one[...] = sigma * (1.0 + pre * (1.0 - sigma))
    pre = nn(hidden, w_second)
    sigma = 1.0 / (1.0 + jnp.exp(-pre))
    hidden = (pre * sigma).astype(BF)
    two[...] = hidden.astype(F32)
    s2[...] = sigma * (1.0 + pre * (1.0 - sigma))
    cols = pl.ds(device_slice(), LANE)
    s1[...] = one[:, cols]
    h2[...] = two[:, cols].astype(BF)
    return hidden


def own_kernel(x, w_first, w_second, w3t, scores, h1, h2, s1, s2, one, two):
    hidden = layers(x[...], w_first[...], w_second[...], h1, h2, s1, s2, one, two)
    scores[...] = nt(w3t[...], hidden).astype(BF)


def peer_kernel(mine, theirs, w_first, w_second, x, h1, h2, s1, s2, one, two):
    half = mine.shape[0]
    core = lax.axis_index("batch")
    x[pl.ds(pl.multiple_of(core * half, half), half), :] = mine[...]
    x[pl.ds(pl.multiple_of((1 - core) * half, half), half), :] = theirs[...]
    layers(x[...], w_first[...], w_second[...], h1, h2, s1, s2, one, two)


def spread(nodes, packed, high, low, label, ids, wts):
    fanout = ids.shape[0]
    targets = ids.shape[1]
    rows = packed.shape[0]
    node_dev = high.shape[0] // 2
    p = packed[...]
    if rows < LANE:
        p = jnp.concatenate([p] * (LANE // rows), axis=0)
    t = p.T
    parts = [t[i * fanout : (i + 1) * fanout] for i in range(4)]
    if rows < LANE:
        lane = lax.broadcasted_iota(jnp.int32, (fanout, LANE), 1)
        coded = jnp.where(lane < rows, parts[0], parts[2])
        wts[...] = jnp.where(lane < rows, parts[1], parts[3])
    else:
        coded = jnp.concatenate([parts[0], parts[2]], axis=1)
        wts[...] = jnp.concatenate([parts[1], parts[3]], axis=1)
    cls = jnp.floor(coded * (1.0 / nodes))
    label[...] = cls[0:1].astype(jnp.int32)
    ids[...] = (coded - cls * nodes).astype(jnp.int32)
    me = lax.axis_index("owner")
    block = 64
    per_side = node_dev // block

    def step(i, carry):
        side = i // per_side
        owner = jnp.where(side == 0, me, me + 1 - 2 * lax.rem(me, 2))
        base = owner * node_dev + lax.rem(i, per_side) * block
        node = lax.broadcasted_iota(jnp.int32, (block, LANE), 0) + base
        at = pl.ds(pl.multiple_of(i * block, block), block)
        for c in range(targets // LANE):
            cols = slice(c * LANE, (c + 1) * LANE)
            total = jnp.zeros((block, LANE), F32)
            for k in range(fanout):
                total += jnp.where(ids[k : k + 1, cols] == node, wts[k : k + 1, cols], 0.0)
            top, rest = split(total)
            high[at, cols] = top
            low[at, cols] = rest
        return carry

    lax.fori_loop(0, 2 * per_side, step, 0)


def logit_kernel(nodes, packed, mine, theirs, high, low, label, part, send, ids, wts):
    spread(nodes, packed, high, low, label, ids, wts)
    n = mine.shape[1]
    total = nn(mine[...], high[:n]) + nn(mine[...], low[:n])
    total += nn(theirs[...], high[n:]) + nn(theirs[...], low[n:])
    part[...] = total
    send[...] = total.astype(BF)


def far_kernel(nodes, packed, high, low, label, ids, wts):
    spread(nodes, packed, high, low, label, ids, wts)


def softmax_kernel(logits, got, label, grad, send, loss):
    v = logits[...] + got[...].astype(F32)
    top = jnp.max(v, axis=0, keepdims=True)
    e = jnp.exp(v - top)
    total = jnp.sum(e, axis=0, keepdims=True)
    hit = lax.broadcasted_iota(jnp.int32, v.shape, 0) == label[...]
    loss[...] = jnp.log(total) + top - jnp.sum(jnp.where(hit, v, 0.0), axis=0, keepdims=True)
    g = e / total - jnp.where(hit, 1.0, 0.0)
    grad[...] = g
    send[...] = g.astype(BF)


def back_kernel(bit, grad, far_grad, high, low, far_high, far_low, x, px, h1, ph1, h2, ph2, s1, ps1, s2, ps2, w3t, w2, send, keep, acc, two):
    top, rest = split(grad[...])
    far = far_grad[...]
    n = x.shape[0]
    depth = x.shape[1]
    hidden = h1.shape[1]
    classes = w3t.shape[0]
    cols = pl.ds(device_slice(), LANE)
    w2_rows = w2[cols, :]
    for side, (x_, h1_, h2_, s1_, s2_) in enumerate(((x, h1, h2, s1, s2), (px, ph1, ph2, ps1, ps2))):
        at = slice(side * n, (side + 1) * n)
        hi, lo, fhi, flo = high[at], low[at], far_high[at], far_low[at]
        g = nt(hi, top) + nt(lo, top) + nt(hi, rest) + nt(fhi, far) + nt(flo, far)
        gt = nt(top, hi) + nt(top, lo) + nt(rest, hi) + nt(far, fhi) + nt(far, flo)
        b2 = nn(g.astype(BF), w3t[...]) * s2_[...]
        two[...] = b2
        b2 = b2.astype(BF)
        b2_cols = two[:, cols].astype(BF)
        b1 = (nt(b2, w2_rows) * s1_[...]).astype(BF)
        first = tn(x_[...], b1)
        second = tn(h1_[...], b2_cols)
        third = nn(gt.astype(BF), h2_[...])
        if side == 0:
            acc[:depth] = first
            acc[depth : depth + hidden] = second
            acc[depth + hidden : depth + hidden + classes] = third
        else:
            acc[:depth] += first
            acc[depth : depth + hidden] += second
            acc[depth + hidden : depth + hidden + classes] += third
    rest_rows = acc.shape[0] - (depth + hidden + classes)
    if rest_rows:
        acc[depth + hidden + classes :] = jnp.zeros((rest_rows, LANE), F32)
    halve(bit, acc, send, keep)


def halve(bit, acc, send, keep):
    rows = acc.shape[0] // 2
    up = lax.rem(lax.axis_index("owner") // bit, 2)
    send[...] = acc[pl.ds(pl.multiple_of((1 - up) * rows, 8), rows), :].astype(BF)
    keep[...] = acc[pl.ds(pl.multiple_of(up * rows, 8), rows), :]


def add_kernel(bit, kept, got, send, keep, acc):
    acc[...] = kept[...] + got[...].astype(F32)
    halve(bit, acc, send, keep)


def last_kernel(kept, got, out):
    out[...] = (kept[...] + got[...].astype(F32)).astype(BF)


def join_kernel(bit, mine, got, out):
    rows = mine.shape[0]
    up = lax.rem(lax.axis_index("owner") // bit, 2)
    out[pl.ds(pl.multiple_of(up * rows, ROW), rows), :] = mine[...]
    out[pl.ds(pl.multiple_of((1 - up) * rows, ROW), rows), :] = got[...]


def place_kernel(mine, across, core, both, first, second, third):
    side = lax.rem(lax.axis_index("owner"), 2)
    half = lax.axis_index("batch")
    depth, hidden, classes = first.shape[0], second.shape[0], third.shape[0]
    for ref, s, h in ((mine, side, half), (across, 1 - side, half), (core, side, 1 - half), (both, 1 - side, 1 - half)):
        cols = pl.ds(pl.multiple_of((2 * s + h) * LANE, LANE), LANE)
        first[:, cols] = ref[:depth]
        second[:, cols] = ref[depth : depth + hidden]
        third[:, cols] = ref[depth + hidden : depth + hidden + classes]


def whole(kernel, outs, scratch, *args, flops=1000000, limit=24):
    return pl.pallas_call(
        kernel,
        out_shape=[jax.ShapeDtypeStruct(shape, kind) for shape, kind in outs],
        in_specs=[pl.BlockSpec(memory_space=pltpu.VMEM)] * len(args),
        out_specs=[pl.BlockSpec(memory_space=pltpu.VMEM)] * len(outs),
        scratch_shapes=[pltpu.VMEM(shape, kind) for shape, kind in scratch],
        compiler_params=pltpu.CompilerParams(vmem_limit_bytes=limit << 20),
        cost_estimate=pl.CostEstimate(flops=flops, bytes_accessed=flops // 512, transcendentals=0),
    )(*args)


def body(features, w_first, w_second, w_third, nbr_ids, nbr_weight, labels):
    owners = lax.axis_size("owner")
    node_dev, depth = features.shape
    hidden, classes = w_third.shape
    rows, fanout = nbr_ids.shape
    nodes = owners * node_dev
    me = lax.axis_index("owner")
    core = lax.axis_index("batch")
    bits = [1 << i for i in range(1, owners.bit_length() - 1)]
    targets = owners * rows

    def over(x, bit):
        return lax.ppermute(x, "owner", [(i, i ^ bit) for i in range(owners)])

    def other_core(x):
        return lax.ppermute(x, "batch", [(0, 1), (1, 0)])

    w3t = w_third.T
    coded = nbr_ids.astype(F32) + (labels * nodes).astype(F32)[:, None]
    packed = jnp.concatenate([coded, nbr_weight], axis=1)
    got = other_core(packed)
    packed = jnp.where(core == 0, jnp.concatenate([packed, got], 1), jnp.concatenate([got, packed], 1))
    for bit in bits:
        got = over(packed, bit)
        up = (me // bit) % 2
        packed = jnp.where(up == 0, jnp.concatenate([packed, got], 0), jnp.concatenate([got, packed], 0))
    far_packed = over(packed, 1)

    kept = [
        ((node_dev, hidden), BF),
        ((node_dev, LANE), BF),
        ((node_dev, LANE), F32),
        ((node_dev, hidden), F32),
    ]
    wide = [((node_dev, hidden), F32)] * 2
    scores, h1, h2, s1, s2 = whole(
        own_kernel, [((classes, node_dev), BF)] + kept, wide, features, w_first, w_second, w3t
    )
    far_scores = over(scores, 1)
    half = node_dev // 2
    peer_half = over(lax.dynamic_slice_in_dim(features, core * half, half, 0), 1)
    peer_rest = other_core(peer_half)
    peer, ph1, ph2, ps1, ps2 = whole(
        peer_kernel, [((node_dev, depth), BF)] + kept, wide, peer_half, peer_rest, w_first, w_second
    )

    big = 24 if owners <= 8 else 56
    maps = [((2 * node_dev, targets), BF), ((2 * node_dev, targets), BF), ((1, targets), jnp.int32)]
    tables = [((fanout, targets), jnp.int32), ((fanout, targets), F32)]
    high, low, label, part, send = whole(
        functools.partial(logit_kernel, nodes),
        maps + [((classes, targets), F32), ((classes, targets), BF)],
        tables,
        packed,
        scores,
        far_scores,
        limit=big,
    )
    far_high, far_low, _ = whole(functools.partial(far_kernel, nodes), maps, tables, far_packed, limit=big)
    for bit in bits[:-1]:
        part = part + over(send, bit).astype(F32)
        send = part.astype(BF)
    grad, grad_send, loss = whole(
        softmax_kernel,
        [((classes, targets), F32), ((classes, targets), BF), ((1, targets), F32)],
        [],
        part,
        over(send, bits[-1]),
        label,
    )
    at = core * (targets // 2) + (me // 2) * rows
    target_loss = lax.dynamic_slice_in_dim(loss[0], at, rows, 0)
    far_grad = over(grad_send, 1)

    step = ROW << len(bits)
    stack = -(-(depth + hidden + classes) // step) * step

    def halves(n):
        return [((n // 2, LANE), BF), ((n // 2, LANE), F32)]

    send, keep = whole(
        functools.partial(back_kernel, bits[0]),
        halves(stack),
        [((stack, LANE), F32), ((node_dev, hidden), F32)],
        grad, far_grad, high, low, far_high, far_low,
        features, peer, h1, ph1, h2, ph2, s1, ps1, s2, ps2, w3t, w_second,
        limit=big,
    )
    size = stack // 2
    for at, bit in enumerate(bits[1:]):
        send, keep = whole(
            functools.partial(add_kernel, bit),
            halves(size),
            [((size, LANE), F32)],
            keep,
            over(send, bits[at]),
        )
        size //= 2
    (out,) = whole(last_kernel, [((size, LANE), BF)], [], keep, over(send, bits[-1]))
    for bit in reversed(bits):
        size *= 2
        (out,) = whole(functools.partial(join_kernel, bit), [((size, LANE), BF)], [], out, over(out, bit))
    across = over(out, 1)
    first, second, third = whole(
        place_kernel,
        [((depth, hidden), BF), ((hidden, hidden), BF), ((classes, hidden), BF)],
        [],
        out,
        across,
        other_core(out),
        other_core(across),
    )
    return first, second, third.T, target_loss


def solution(mesh):
    in_specs = (
        P("owner", None),
        P(),
        P(),
        P(),
        P(("groups", "owner", "batch"), None),
        P(("groups", "owner", "batch"), None),
        P(("groups", "owner", "batch")),
    )
    out_specs = (
        P("groups", None),
        P("groups", None),
        P("groups", None),
        P(("groups", "owner", "batch")),
    )
    return jax.shard_map(body, mesh=mesh, in_specs=in_specs, out_specs=out_specs, check_vma=False)
```

```python
import functools
import jax
import jax.numpy as jnp
from jax import lax
from jax.experimental import pallas as pl
from jax.experimental.pallas import tpu as pltpu
from jax.sharding import PartitionSpec as P

BF = jnp.bfloat16
F32 = jnp.float32
ROW = 16
LANE = 128


def nn(a, b):
    return lax.dot_general(a, b, (((1,), (0,)), ((), ())), preferred_element_type=F32)


def nt(a, b):
    return lax.dot_general(a, b, (((1,), (1,)), ((), ())), preferred_element_type=F32)


def split(v):
    high = v.astype(BF)
    return high, (v - high.astype(F32)).astype(BF)


def device_slice():
    place = lax.rem(lax.axis_index("owner"), 2) * 2 + lax.axis_index("batch")
    return pl.multiple_of(place * LANE, LANE)


def activate(pre):
    sigma = 1.0 / (1.0 + jnp.exp(-pre))
    return (pre * sigma).astype(BF), sigma * (1.0 + pre * (1.0 - sigma))


def launch(sem, pairs):
    copies = [pltpu.make_async_copy(a, b, sem.at[i]) for i, (a, b) in enumerate(pairs)]
    for c in copies:
        c.start()
    return copies


def pack_kernel(nodes, ids, wts, labels, out):
    rows, fanout = ids.shape
    shape = (rows, rows)
    same = lax.broadcasted_iota(jnp.int32, shape, 0) == lax.broadcasted_iota(jnp.int32, shape, 1)
    label = jnp.sum(jnp.where(same, labels[...].astype(F32), 0.0), axis=1, keepdims=True)
    out[:, :fanout] = ids[...].astype(F32) + label * nodes
    out[:, fanout:] = wts[...]


def own_kernel(x_hbm, w1_hbm, w2_hbm, w3_hbm, after, scores, half, x, w1, w2, w3, sem):
    del after
    into = launch(sem, ((x_hbm, x), (w1_hbm, w1), (w2_hbm, w2), (w3_hbm, w3)))
    into[0].wait()
    rows = half.shape[0]
    half[...] = x[pl.ds(pl.multiple_of(lax.axis_index("batch") * rows, ROW), rows), :]
    into[1].wait()
    hidden = activate(nn(x[...], w1[...]))[0]
    into[2].wait()
    hidden = activate(nn(hidden, w2[...]))[0]
    into[3].wait()
    scores[...] = nt(w3[...], hidden).astype(BF)


def layers(x, w1, w2, xt, h1t, h2, s1, s2, one, two):
    cols = pl.ds(device_slice(), LANE)
    rows = x[...]
    xt[...] = rows.T
    hidden, slope = activate(nn(rows, w1[...]))
    h1t[...] = hidden.T
    one[...] = slope
    s1[...] = one[:, cols]
    hidden, slope = activate(nn(hidden, w2[...]))
    two[...] = hidden
    s2[...] = slope
    h2[...] = two[:, cols]


def again_kernel(x, w1, w2, after, xt, h1t, h2, s1, s2, one, two):
    del after
    layers(x, w1, w2, xt, h1t, h2, s1, s2, one, two)


def peer_kernel(mine, theirs, w1, w2, xt, h1t, h2, s1, s2, x, one, two):
    half = mine.shape[0]
    core = lax.axis_index("batch")
    x[pl.ds(pl.multiple_of(core * half, half), half), :] = mine[...]
    x[pl.ds(pl.multiple_of((1 - core) * half, half), half), :] = theirs[...]
    layers(x, w1, w2, xt, h1t, h2, s1, s2, one, two)


def spread(nodes, packed, high, low, label, ids, wts):
    fanout = ids.shape[0]
    targets = ids.shape[1]
    rows = packed.shape[0]
    node_dev = high.shape[0] // 2
    p = packed[...]
    if rows < LANE:
        p = jnp.concatenate([p] * (LANE // rows), axis=0)
    t = p.T
    parts = [t[i * fanout : (i + 1) * fanout] for i in range(4)]
    if rows < LANE:
        lane = lax.broadcasted_iota(jnp.int32, (fanout, LANE), 1)
        coded = jnp.where(lane < rows, parts[0], parts[2])
        wts[...] = jnp.where(lane < rows, parts[1], parts[3])
    else:
        coded = jnp.concatenate([parts[0], parts[2]], axis=1)
        wts[...] = jnp.concatenate([parts[1], parts[3]], axis=1)
    cls = jnp.floor(coded * (1.0 / nodes))
    label[...] = cls[0:1].astype(jnp.int32)
    ids[...] = (coded - cls * nodes).astype(jnp.int32)
    me = lax.axis_index("owner")
    block = 64
    per_side = node_dev // block

    def step(i, carry):
        side = i // per_side
        owner = jnp.where(side == 0, me, me + 1 - 2 * lax.rem(me, 2))
        base = owner * node_dev + lax.rem(i, per_side) * block
        node = lax.broadcasted_iota(jnp.int32, (block, LANE), 0) + base
        at = pl.ds(pl.multiple_of(i * block, block), block)
        for c in range(targets // LANE):
            cols = slice(c * LANE, (c + 1) * LANE)
            total = jnp.zeros((block, LANE), F32)
            for k in range(fanout):
                total += jnp.where(ids[k : k + 1, cols] == node, wts[k : k + 1, cols], 0.0)
            top, rest = split(total)
            high[at, cols] = top
            low[at, cols] = rest
        return carry

    lax.fori_loop(0, 2 * per_side, step, 0)


def logit_kernel(mine, theirs, high, low, part, send):
    n = mine.shape[1]
    total = nn(mine[...], high[:n]) + nn(mine[...], low[:n])
    total += nn(theirs[...], high[n:]) + nn(theirs[...], low[n:])
    part[...] = total
    send[...] = total.astype(BF)


def spread_kernel(nodes, packed, high, low, label, ids, wts):
    spread(nodes, packed, high, low, label, ids, wts)


def softmax_kernel(logits, got, label, grad, send, loss):
    v = logits[...] + got[...].astype(F32)
    top = jnp.max(v, axis=0, keepdims=True)
    e = jnp.exp(v - top)
    total = jnp.sum(e, axis=0, keepdims=True)
    hit = lax.broadcasted_iota(jnp.int32, v.shape, 0) == label[...]
    loss[...] = jnp.log(total) + top - jnp.sum(jnp.where(hit, v, 0.0), axis=0, keepdims=True)
    g = e / total - jnp.where(hit, 1.0, 0.0)
    grad[...] = g
    send[...] = g.astype(BF)


def back_kernel(bit, grad, far_grad, high, low, far_high, far_low, xt, pxt, h1t, ph1t, h2, ph2, s1, ps1, s2, ps2, w3t, w2, send, keep, acc, two):
    top, rest = split(grad[...])
    far = far_grad[...]
    depth, n = xt.shape
    hidden = h1t.shape[0]
    classes = w3t.shape[0]
    cols = pl.ds(device_slice(), LANE)
    w2_rows = w2[cols, :]
    for side, (x_, h1_, h2_, s1_, s2_) in enumerate(((xt, h1t, h2, s1, s2), (pxt, ph1t, ph2, ps1, ps2))):
        at = slice(side * n, (side + 1) * n)
        hi, lo, fhi, flo = high[at], low[at], far_high[at], far_low[at]
        g = nt(hi, top) + nt(lo, top) + nt(hi, rest) + nt(fhi, far) + nt(flo, far)
        gt = nt(top, hi) + nt(top, lo) + nt(rest, hi) + nt(far, fhi) + nt(far, flo)
        b2 = nn(g.astype(BF), w3t[...]) * s2_[...]
        two[...] = b2
        b2 = b2.astype(BF)
        b2_cols = two[:, cols].astype(BF)
        b1 = (nt(b2, w2_rows) * s1_[...]).astype(BF)
        first = nn(x_[...], b1)
        second = nn(h1_[...], b2_cols)
        third = nn(gt.astype(BF), h2_[...])
        if side == 0:
            acc[:depth] = first
            acc[depth : depth + hidden] = second
            acc[depth + hidden : depth + hidden + classes] = third
        else:
            acc[:depth] += first
            acc[depth : depth + hidden] += second
            acc[depth + hidden : depth + hidden + classes] += third
    rest_rows = acc.shape[0] - (depth + hidden + classes)
    if rest_rows:
        acc[depth + hidden + classes :] = jnp.zeros((rest_rows, LANE), F32)
    halve(bit, acc, send, keep)


def halve(bit, acc, send, keep):
    rows = acc.shape[0] // 2
    up = lax.rem(lax.axis_index("owner") // bit, 2)
    send[...] = acc[pl.ds(pl.multiple_of((1 - up) * rows, 8), rows), :].astype(BF)
    keep[...] = acc[pl.ds(pl.multiple_of(up * rows, 8), rows), :]


def add_kernel(bit, kept, got, send, keep, acc):
    acc[...] = kept[...] + got[...].astype(F32)
    halve(bit, acc, send, keep)


def last_kernel(kept, got, out):
    out[...] = (kept[...] + got[...].astype(F32)).astype(BF)


def join_kernel(bit, mine, got, out):
    rows = mine.shape[0]
    up = lax.rem(lax.axis_index("owner") // bit, 2)
    out[pl.ds(pl.multiple_of(up * rows, ROW), rows), :] = mine[...]
    out[pl.ds(pl.multiple_of((1 - up) * rows, ROW), rows), :] = got[...]


def place_kernel(bit, *refs):
    halves, outs = refs[:8], refs[8:]
    me = lax.axis_index("owner")
    side = lax.rem(me, 2)
    core = lax.axis_index("batch")
    up = lax.rem(me // bit, 2)
    rows = halves[0].shape[0]

    def fill(order):
        for i, (s, h) in enumerate(((side, core), (1 - side, core), (side, 1 - core), (1 - side, 1 - core))):
            cols = pl.ds(pl.multiple_of((2 * s + h) * LANE, LANE), LANE)
            for j in range(2):
                ref = halves[2 * i + order[j]]
                top = 0
                for out in outs:
                    low, high = max(top, j * rows), min(top + out.shape[0], (j + 1) * rows)
                    if low < high:
                        out[low - top : high - top, cols] = ref[low - j * rows : high - j * rows]
                    top += out.shape[0]

    @pl.when(up == 0)
    def _():
        fill((0, 1))

    @pl.when(up == 1)
    def _():
        fill((1, 0))


def whole(kernel, outs, scratch, *args, flops=1000000, limit=24, far_in=(), far_out=()):
    def spec(i, far):
        return pl.BlockSpec(memory_space=pltpu.HBM if i in far else pltpu.VMEM)

    return pl.pallas_call(
        kernel,
        out_shape=[jax.ShapeDtypeStruct(shape, kind) for shape, kind in outs],
        in_specs=[spec(i, far_in) for i in range(len(args))],
        out_specs=[spec(i, far_out) for i in range(len(outs))],
        scratch_shapes=[
            pltpu.SemaphoreType.DMA((s,)) if isinstance(s, int) else pltpu.VMEM(*s) for s in scratch
        ],
        compiler_params=pltpu.CompilerParams(vmem_limit_bytes=limit << 20),
        cost_estimate=pl.CostEstimate(flops=flops, bytes_accessed=flops // 512, transcendentals=0),
    )(*args)


def body(features, w_first, w_second, w_third, nbr_ids, nbr_weight, labels):
    owners = lax.axis_size("owner")
    node_dev, depth = features.shape
    hidden, classes = w_third.shape
    rows, fanout = nbr_ids.shape
    nodes = owners * node_dev
    me = lax.axis_index("owner")
    core = lax.axis_index("batch")
    bits = [1 << i for i in range(1, owners.bit_length() - 1)]
    targets = owners * rows

    def over(x, bit):
        return lax.ppermute(x, "owner", [(i, i ^ bit) for i in range(owners)])

    def other_core(x):
        return lax.ppermute(x, "batch", [(0, 1), (1, 0)])

    w3t = w_third.T
    (packed,) = whole(
        functools.partial(pack_kernel, nodes),
        [((rows, 2 * fanout), F32)],
        [],
        nbr_ids,
        nbr_weight,
        labels.reshape(1, rows),
    )
    got = other_core(packed)
    packed = jnp.where(core == 0, jnp.concatenate([packed, got], 1), jnp.concatenate([got, packed], 1))
    half = node_dev // 2
    w1_type, w2_type, x_type = (w_first.shape, BF), (w_second.shape, BF), (features.shape, BF)
    scores, my_half = whole(
        own_kernel,
        [((classes, node_dev), BF), ((half, depth), BF)],
        [x_type, w1_type, w2_type, (w3t.shape, BF), 4],
        features,
        w_first,
        w_second,
        w3t,
        packed,
        flops=2000000000,
        limit=60,
        far_in=range(5),
    )
    for bit in bits:
        got = over(packed, bit)
        if bit == bits[0]:
            got, scores = lax.optimization_barrier((got, scores))
        up = (me // bit) % 2
        packed = jnp.where(up == 0, jnp.concatenate([packed, got], 0), jnp.concatenate([got, packed], 0))
    far_packed = over(packed, 1)
    far_scores = over(scores, 1)
    my_half, packed = lax.optimization_barrier((my_half, packed))
    peer_half = over(my_half, 1)

    big = 24 if owners <= 8 else 48
    maps = [((2 * node_dev, targets), BF), ((2 * node_dev, targets), BF), ((1, targets), jnp.int32)]
    tables = [((fanout, targets), jnp.int32), ((fanout, targets), F32)]
    spread_call = functools.partial(whole, functools.partial(spread_kernel, nodes), maps, tables, limit=big, flops=1000000000)
    high, low, label = spread_call(packed)
    part, send = whole(
        logit_kernel,
        [((classes, targets), F32), ((classes, targets), BF)],
        [],
        scores,
        far_scores,
        high,
        low,
        limit=big,
    )
    far_high, far_low, _ = spread_call(far_packed)
    for bit in bits[:-1]:
        got = over(send, bit)
        if bit == bits[0]:
            got, far_high, far_low = lax.optimization_barrier((got, far_high, far_low))
        part = part + got.astype(F32)
        send = part.astype(BF)
    kept = [
        ((depth, node_dev), BF),
        ((hidden, node_dev), BF),
        ((node_dev, LANE), BF),
        ((node_dev, LANE), F32),
        ((node_dev, hidden), F32),
    ]
    work = [((node_dev, hidden), F32), ((node_dev, hidden), BF)]
    xt, h1t, h2, s1, s2 = whole(
        again_kernel, kept, work, features, w_first, w_second, send, flops=2000000000, far_in=(3,)
    )
    got = over(send, bits[-1])
    peer_half = lax.optimization_barrier((peer_half, got))[0]
    peer_rest = other_core(peer_half)
    pxt, ph1t, ph2, ps1, ps2 = whole(
        peer_kernel,
        kept,
        [x_type] + work,
        peer_half,
        peer_rest,
        w_first,
        w_second,
        flops=2000000000,
    )
    got = lax.optimization_barrier((got, s1))[0]
    grad, grad_send, loss = whole(
        softmax_kernel,
        [((classes, targets), F32), ((classes, targets), BF), ((1, targets), F32)],
        [],
        part,
        got,
        label,
    )
    at = core * (targets // 2) + (me // 2) * rows
    target_loss = lax.dynamic_slice_in_dim(loss[0], at, rows, 0)
    far_grad = over(grad_send, 1)

    step = ROW << len(bits)
    stack = -(-(depth + hidden + classes) // step) * step

    def halves(n):
        return [((n // 2, LANE), BF), ((n // 2, LANE), F32)]

    send, keep = whole(
        functools.partial(back_kernel, bits[0]),
        halves(stack),
        [((stack, LANE), F32), ((node_dev, hidden), F32)],
        grad, far_grad, high, low, far_high, far_low,
        xt, pxt, h1t, ph1t, h2, ph2, s1, ps1, s2, ps2, w3t, w_second,
        limit=big,
    )
    size = stack // 2
    for at, bit in enumerate(bits[1:]):
        send, keep = whole(
            functools.partial(add_kernel, bit),
            halves(size),
            [((size, LANE), F32)],
            keep,
            over(send, bits[at]),
        )
        size //= 2
    (out,) = whole(last_kernel, [((size, LANE), BF)], [], keep, over(send, bits[-1]))
    for bit in reversed(bits[1:]):
        size *= 2
        (out,) = whole(functools.partial(join_kernel, bit), [((size, LANE), BF)], [], out, over(out, bit))
    pair = (out, over(out, bits[0]))
    across = [over(p, 1) for p in pair]
    cores = [other_core(p) for p in pair]
    both = [other_core(p) for p in across]
    first, second, third = whole(
        functools.partial(place_kernel, bits[0]),
        [((depth, hidden), BF), ((hidden, hidden), BF), ((classes, hidden), BF)],
        [],
        *pair,
        *across,
        *cores,
        *both,
    )
    return first, second, third.T, target_loss


def solution(mesh):
    in_specs = (
        P("owner", None),
        P(),
        P(),
        P(),
        P(("groups", "owner", "batch"), None),
        P(("groups", "owner", "batch"), None),
        P(("groups", "owner", "batch")),
    )
    out_specs = (
        P("groups", None),
        P("groups", None),
        P("groups", None),
        P(("groups", "owner", "batch")),
    )
    return jax.shard_map(body, mesh=mesh, in_specs=in_specs, out_specs=out_specs, check_vma=False)
```

```python
import functools
import jax
import jax.numpy as jnp
from jax import lax
from jax.experimental import pallas as pl
from jax.experimental.pallas import tpu as pltpu
from jax.sharding import PartitionSpec as P

BF = jnp.bfloat16
F32 = jnp.float32
ROW = 16
LANE = 128
PACK = 16


def nn(a, b):
    return lax.dot_general(a, b, (((1,), (0,)), ((), ())), preferred_element_type=F32)


def nt(a, b):
    return lax.dot_general(a, b, (((1,), (1,)), ((), ())), preferred_element_type=F32)


def split(v):
    high = v.astype(BF)
    return high, (v - high.astype(F32)).astype(BF)


def device_slice():
    place = lax.rem(lax.axis_index("owner"), 2) * 2 + lax.axis_index("batch")
    return pl.multiple_of(place * LANE, LANE)


def activate(pre):
    sigma = 0.5 * jnp.tanh(0.5 * pre) + 0.5
    return (pre * sigma).astype(BF), sigma * (1.0 + pre * (1.0 - sigma))


def launch(sem, pairs):
    copies = [pltpu.make_async_copy(a, b, sem.at[i]) for i, (a, b) in enumerate(pairs)]
    for c in copies:
        c.start()
    return copies


def pack_kernel(nodes, ids_hbm, wts_hbm, labels_hbm, x_hbm, w1_hbm, w2_hbm, w3_hbm, out, half, x, w1, w2, w3, ids, wts, labels, sem):
    rows, fanout = ids.shape
    part = half.shape[0]
    mine = x_hbm.at[pl.ds(pl.multiple_of(lax.axis_index("batch") * part, ROW), part), :]
    small = ((labels_hbm, labels), (ids_hbm, ids), (wts_hbm, wts))
    into = launch(sem, small + ((mine, half), (x_hbm, x), (w1_hbm, w1), (w2_hbm, w2), (w3_hbm, w3)))
    for c in into[:3]:
        c.wait()
    shape = (rows, rows)
    same = lax.broadcasted_iota(jnp.int32, shape, 0) == lax.broadcasted_iota(jnp.int32, shape, 1)
    label = jnp.sum(jnp.where(same, labels[...].astype(F32), 0.0), axis=1, keepdims=True)
    out[:, :fanout] = ids[...].astype(F32) + label * nodes
    out[:, fanout:] = wts[...]
    for c in into[3:]:
        c.wait()


def own_kernel(x, w1, w2, w3, after, scores):
    del after
    hidden = activate(nn(x[...], w1[...]))[0]
    hidden = activate(nn(hidden, w2[...]))[0]
    scores[...] = nt(w3[...], hidden).astype(BF)


def layers(x, w1, w2, xt, h1t, h2, s1, s2, one, two):
    cols = pl.ds(device_slice(), LANE)
    rows = x[...]
    xt[...] = rows.T
    hidden, slope = activate(nn(rows, w1[...]))
    h1t[...] = hidden.T
    one[...] = slope
    s1[...] = one[:, cols]
    hidden, slope = activate(nn(hidden, w2[...]))
    two[...] = hidden
    s2[...] = slope
    h2[...] = two[:, cols]


def again_kernel(x, w1, w2, after, xt, h1t, h2, s1, s2, one, two):
    del after
    layers(x, w1, w2, xt, h1t, h2, s1, s2, one, two)


def peer_kernel(mine, theirs, w1, w2, xt, h1t, h2, s1, s2, x, one, two):
    half = mine.shape[0]
    core = lax.axis_index("batch")
    x[pl.ds(pl.multiple_of(core * half, half), half), :] = mine[...]
    x[pl.ds(pl.multiple_of((1 - core) * half, half), half), :] = theirs[...]
    layers(x, w1, w2, xt, h1t, h2, s1, s2, one, two)


def spread(nodes, packed, high, low, label, ids, wts):
    fanout = ids.shape[0]
    targets = ids.shape[1]
    rows = packed.shape[0]
    node_dev = high.shape[0] // 2
    p = packed[...]
    if rows < LANE:
        p = jnp.concatenate([p] * (LANE // rows), axis=0)
    t = p.T
    parts = [t[i * fanout : (i + 1) * fanout] for i in range(4)]
    if rows < LANE:
        lane = lax.broadcasted_iota(jnp.int32, (fanout, LANE), 1)
        coded = jnp.where(lane < rows, parts[0], parts[2])
        wts[...] = jnp.where(lane < rows, parts[1], parts[3])
    else:
        coded = jnp.concatenate([parts[0], parts[2]], axis=1)
        wts[...] = jnp.concatenate([parts[1], parts[3]], axis=1)
    cls = jnp.floor(coded * (1.0 / nodes))
    label[...] = cls[0:1].astype(jnp.int32)
    ids[...] = (coded - cls * nodes).astype(jnp.int32)
    me = lax.axis_index("owner")
    block = 64
    per_side = node_dev // block

    def step(i, carry):
        side = i // per_side
        owner = jnp.where(side == 0, me, me + 1 - 2 * lax.rem(me, 2))
        base = owner * node_dev + lax.rem(i, per_side) * block
        node = lax.broadcasted_iota(jnp.int32, (block, LANE), 0) + base
        at = pl.ds(pl.multiple_of(i * block, block), block)
        for c in range(targets // LANE):
            cols = slice(c * LANE, (c + 1) * LANE)
            total = jnp.zeros((block, LANE), F32)
            for k in range(fanout):
                total += jnp.where(ids[k : k + 1, cols] == node, wts[k : k + 1, cols], 0.0)
            top, rest = split(total)
            high[at, cols] = top
            low[at, cols] = rest
        return carry

    lax.fori_loop(0, 2 * per_side, step, 0)


def logit_kernel(mine, theirs, high, low, part, send):
    n = mine.shape[1]
    total = nn(mine[...], high[:n]) + nn(mine[...], low[:n])
    total += nn(theirs[...], high[n:]) + nn(theirs[...], low[n:])
    part[...] = total
    send[...] = total.astype(BF)


def spread_kernel(nodes, packed, high, low, label, ids, wts):
    spread(nodes, packed, high, low, label, ids, wts)


def softmax_kernel(logits, got, label, grad, send, loss):
    v = logits[...] + got[...].astype(F32)
    top = jnp.max(v, axis=0, keepdims=True)
    e = jnp.exp(v - top)
    total = jnp.sum(e, axis=0, keepdims=True)
    hit = lax.broadcasted_iota(jnp.int32, v.shape, 0) == label[...]
    loss[...] = jnp.log(total) + top - jnp.sum(jnp.where(hit, v, 0.0), axis=0, keepdims=True)
    g = e / total - jnp.where(hit, 1.0, 0.0)
    grad[...] = g
    send[...] = g.astype(BF)


def back_kernel(bit, grad, far_grad, high, low, far_high, far_low, xt, pxt, h1t, ph1t, h2, ph2, s1, ps1, s2, ps2, w3t, w2, send, keep, acc, two):
    top, rest = split(grad[...])
    far = far_grad[...]
    depth, n = xt.shape
    hidden = h1t.shape[0]
    classes = w3t.shape[0]
    cols = pl.ds(device_slice(), LANE)
    w2_rows = w2[cols, :]
    sides = (slice(0, n), slice(n, 2 * n))
    left = [jnp.concatenate([high[at], low[at], high[at], far_high[at], far_low[at]], axis=1) for at in sides]
    right = jnp.concatenate([top, top, rest, far, far], axis=1)
    g = [nt(v, right).astype(BF) for v in left]
    b2 = [(nn(v, w3t[...]) * s[...]).astype(BF) for v, s in zip(g, (s2, ps2))]
    two[0] = b2[0]
    two[1] = b2[1]
    b1 = [(nt(v, w2_rows) * s[...]).astype(BF) for v, s in zip(b2, (s1, ps1))]
    gt = [nt(right, v).astype(BF) for v in left]
    acc[depth + hidden : depth + hidden + classes] = nn(gt[0], h2[...]) + nn(gt[1], ph2[...])
    acc[depth : depth + hidden] = nn(h1t[...], two[0, :, cols]) + nn(ph1t[...], two[1, :, cols])
    acc[:depth] = nn(xt[...], b1[0]) + nn(pxt[...], b1[1])
    blank = acc.shape[0] - (depth + hidden + classes)
    if blank:
        acc[depth + hidden + classes :] = jnp.zeros((blank, LANE), F32)
    halve(bit, acc, send, keep)


def halve(bit, acc, send, keep):
    rows = acc.shape[0] // 2
    up = lax.rem(lax.axis_index("owner") // bit, 2)
    send[...] = acc[pl.ds(pl.multiple_of((1 - up) * rows, 8), rows), :].astype(BF)
    keep[...] = acc[pl.ds(pl.multiple_of(up * rows, 8), rows), :]


def add_kernel(bit, kept, got, send, keep, acc):
    acc[...] = kept[...] + got[...].astype(F32)
    halve(bit, acc, send, keep)


def sum_kernel(kept, got, out):
    out[...] = (kept[...].astype(F32) + got[...].astype(F32)).astype(BF)


def join_kernel(bit, mine, got, out):
    rows = mine.shape[0]
    up = lax.rem(lax.axis_index("owner") // bit, 2)
    out[pl.ds(pl.multiple_of(up * rows, ROW), rows), :] = mine[...]
    out[pl.ds(pl.multiple_of((1 - up) * rows, ROW), rows), :] = got[...]


def fill(order, halves, sides, outs):
    rows = halves[0].shape[0]
    for i, (s, h) in enumerate(sides):
        cols = pl.ds(pl.multiple_of((2 * s + h) * LANE, LANE), LANE)
        for j in range(2):
            ref = halves[2 * i + order[j]]
            if ref is None:
                continue
            top = 0
            for out in outs:
                low, high = max(top, j * rows), min(top + out.shape[0], (j + 1) * rows)
                if low < high:
                    out[low - top : high - top, cols] = ref[low - j * rows : high - j * rows]
                top += out.shape[0]


def place_kernel(bit, *refs):
    halves, outs = refs[:8], refs[8:]
    me = lax.axis_index("owner")
    side = lax.rem(me, 2)
    core = lax.axis_index("batch")
    up = lax.rem(me // bit, 2)
    sides = ((side, core), (1 - side, core), (side, 1 - core), (1 - side, 1 - core))

    @pl.when(up == 0)
    def _():
        fill((0, 1), halves, sides, outs)

    @pl.when(up == 1)
    def _():
        fill((1, 0), halves, sides, outs)


def whole(kernel, outs, scratch, *args, flops=1000000, limit=24, far_in=(), far_out=()):
    def spec(i, far):
        return pl.BlockSpec(memory_space=pltpu.HBM if i in far else pltpu.VMEM)

    args = [
        pltpu.with_memory_space_constraint(x, pltpu.HBM) if i in far_in else x for i, x in enumerate(args)
    ]
    return pl.pallas_call(
        kernel,
        out_shape=[jax.ShapeDtypeStruct(shape, kind) for shape, kind in outs],
        in_specs=[spec(i, far_in) for i in range(len(args))],
        out_specs=[spec(i, far_out) for i in range(len(outs))],
        scratch_shapes=[
            pltpu.SemaphoreType.DMA((s,)) if isinstance(s, int) else pltpu.VMEM(*s) for s in scratch
        ],
        compiler_params=pltpu.CompilerParams(vmem_limit_bytes=limit << 20),
        cost_estimate=pl.CostEstimate(flops=flops, bytes_accessed=flops // 512, transcendentals=0),
    )(*args)


def body(features, w_first, w_second, w_third, nbr_ids, nbr_weight, labels):
    owners = lax.axis_size("owner")
    node_dev, depth = features.shape
    hidden, classes = w_third.shape
    rows, fanout = nbr_ids.shape
    nodes = owners * node_dev
    me = lax.axis_index("owner")
    core = lax.axis_index("batch")
    bits = [1 << i for i in range(1, owners.bit_length() - 1)]
    targets = owners * rows

    def over(x, bit):
        return lax.ppermute(x, "owner", [(i, i ^ bit) for i in range(owners)])

    def other_core(x):
        return lax.ppermute(x, "batch", [(0, 1), (1, 0)])

    w3t = w_third.T
    half = node_dev // 2
    w1_type, w2_type, x_type = (w_first.shape, BF), (w_second.shape, BF), (features.shape, BF)
    packed, my_half, features, w_first, w_second, w3t = whole(
        functools.partial(pack_kernel, nodes),
        [((rows, 2 * fanout), F32), ((half, depth), BF), x_type, w1_type, w2_type, (w3t.shape, BF)],
        [((rows, fanout), jnp.int32), ((rows, fanout), F32), ((1, rows), jnp.int32), 8],
        nbr_ids,
        nbr_weight,
        labels.reshape(1, rows),
        features,
        w_first,
        w_second,
        w3t,
        limit=PACK,
        far_in=range(7),
    )
    peer_half = over(my_half, 1)
    got = other_core(packed)
    packed = jnp.where(core == 0, jnp.concatenate([packed, got], 1), jnp.concatenate([got, packed], 1))
    (scores,) = whole(
        own_kernel,
        [((classes, node_dev), BF)],
        [],
        features,
        w_first,
        w_second,
        w3t,
        packed,
        flops=2000000000,
        limit=16,
        far_in=(4,),
    )
    for bit in bits:
        got = over(packed, bit)
        if bit == bits[0]:
            got, scores = lax.optimization_barrier((got, scores))
        up = (me // bit) % 2
        packed = jnp.where(up == 0, jnp.concatenate([packed, got], 0), jnp.concatenate([got, packed], 0))
    far_scores = over(scores, 1)

    big = 24 if owners <= 8 else 48
    maps = [((2 * node_dev, targets), BF), ((2 * node_dev, targets), BF), ((1, targets), jnp.int32)]
    tables = [((fanout, targets), jnp.int32), ((fanout, targets), F32)]
    spread_call = functools.partial(whole, functools.partial(spread_kernel, nodes), maps, tables, limit=big, flops=1000000000)
    high, low, label = spread_call(packed)
    part, send = whole(
        logit_kernel,
        [((classes, targets), F32), ((classes, targets), BF)],
        [],
        scores,
        far_scores,
        high,
        low,
        limit=big,
    )
    kept = [
        ((depth, node_dev), BF),
        ((hidden, node_dev), BF),
        ((node_dev, LANE), BF),
        ((node_dev, LANE), F32),
        ((node_dev, hidden), F32),
    ]
    work = [((node_dev, hidden), F32), ((node_dev, hidden), BF)]
    packed = lax.optimization_barrier((packed, send))[0]
    far_packed = over(packed, 1)
    peer_half = lax.optimization_barrier((peer_half, send))[0]
    peer_rest = other_core(peer_half)
    xt, h1t, h2, s1, s2 = whole(
        again_kernel, kept, work, features, w_first, w_second, send, flops=2000000000, far_in=(3,)
    )
    for bit in bits[:-1]:
        got = over(send, bit)
        if bit == bits[0]:
            got = lax.optimization_barrier((got, s1))[0]
        part = part + got.astype(F32)
        send = part.astype(BF)
    far_packed = lax.optimization_barrier((far_packed, send))[0]
    far_high, far_low, _ = spread_call(far_packed)
    got = over(send, bits[-1])
    peer_rest = lax.optimization_barrier((peer_rest, got))[0]
    pxt, ph1t, ph2, ps1, ps2 = whole(
        peer_kernel,
        kept,
        [x_type] + work,
        peer_half,
        peer_rest,
        w_first,
        w_second,
        flops=2000000000,
    )
    got = lax.optimization_barrier((got, far_high))[0]
    grad, grad_send, loss = whole(
        softmax_kernel,
        [((classes, targets), F32), ((classes, targets), BF), ((1, targets), F32)],
        [],
        part,
        got,
        label,
    )
    at = core * (targets // 2) + (me // 2) * rows
    target_loss = lax.dynamic_slice_in_dim(loss[0], at, rows, 0)
    far_grad = over(grad_send, 1)

    step = ROW << (len(bits) - 1)
    stack = -(-(depth + hidden + classes) // step) * step

    def halves(n):
        return [((n // 2, LANE), BF), ((n // 2, LANE), F32)]

    send, keep = whole(
        functools.partial(back_kernel, bits[0]),
        halves(stack),
        [((stack, LANE), F32), ((2, node_dev, hidden), BF)],
        grad, far_grad, high, low, far_high, far_low,
        xt, pxt, h1t, ph1t, h2, ph2, s1, ps1, s2, ps2, w3t, w_second,
        limit=big,
    )
    size = stack // 2
    for at, bit in enumerate(bits[1:-1]):
        send, keep = whole(
            functools.partial(add_kernel, bit),
            halves(size),
            [((size, LANE), F32)],
            keep,
            over(send, bits[at]),
        )
        size //= 2
    for mine, bit in ((keep, bits[-2]), (None, bits[-1])):
        got = over(send, bit)
        (send,) = whole(sum_kernel, [((size, LANE), BF)], [], send if mine is None else mine, got)
    out = send
    for bit in reversed(bits[1:-1]):
        size *= 2
        (out,) = whole(functools.partial(join_kernel, bit), [((size, LANE), BF)], [], out, over(out, bit))
    pair = (out, over(out, bits[0]))
    across = [over(p, 1) for p in pair]
    cores = [other_core(p) for p in pair]
    both = [other_core(p) for p in across]
    first, second, third = whole(
        functools.partial(place_kernel, bits[0]),
        [((depth, hidden), BF), ((hidden, hidden), BF), ((classes, hidden), BF)],
        [],
        *pair,
        *across,
        *cores,
        *both,
    )
    return first, second, third.T, target_loss


def solution(mesh):
    in_specs = (
        P("owner", None),
        P(),
        P(),
        P(),
        P(("groups", "owner", "batch"), None),
        P(("groups", "owner", "batch"), None),
        P(("groups", "owner", "batch")),
    )
    out_specs = (
        P("groups", None),
        P("groups", None),
        P("groups", None),
        P(("groups", "owner", "batch")),
    )
    return jax.shard_map(body, mesh=mesh, in_specs=in_specs, out_specs=out_specs, check_vma=False)
```

```python
import functools
import jax
import jax.numpy as jnp
from jax import lax
from jax.experimental import pallas as pl
from jax.experimental.pallas import tpu as pltpu
from jax.sharding import PartitionSpec as P

BF = jnp.bfloat16
F32 = jnp.float32
ROW = 16
LANE = 128
PACK = 16


def nn(a, b):
    return lax.dot_general(a, b, (((1,), (0,)), ((), ())), preferred_element_type=F32)


def nt(a, b):
    return lax.dot_general(a, b, (((1,), (1,)), ((), ())), preferred_element_type=F32)


def split(v):
    high = v.astype(BF)
    return high, (v - high.astype(F32)).astype(BF)


def device_slice():
    place = lax.rem(lax.axis_index("owner"), 2) * 2 + lax.axis_index("batch")
    return pl.multiple_of(place * LANE, LANE)


def activate(pre):
    sigma = 0.5 * jnp.tanh(0.5 * pre) + 0.5
    return (pre * sigma).astype(BF), sigma * (1.0 + pre * (1.0 - sigma))


def launch(sem, pairs):
    copies = [pltpu.make_async_copy(a, b, sem.at[i]) for i, (a, b) in enumerate(pairs)]
    for c in copies:
        c.start()
    return copies


def pack_kernel(nodes, ids_hbm, wts_hbm, labels_hbm, x_hbm, out, half, ids, wts, labels, sem):
    rows, fanout = ids.shape
    part = half.shape[0]
    mine = x_hbm.at[pl.ds(pl.multiple_of(lax.axis_index("batch") * part, ROW), part), :]
    into = launch(sem, ((labels_hbm, labels), (ids_hbm, ids), (wts_hbm, wts), (mine, half)))
    for c in into[:3]:
        c.wait()
    shape = (rows, rows)
    same = lax.broadcasted_iota(jnp.int32, shape, 0) == lax.broadcasted_iota(jnp.int32, shape, 1)
    label = jnp.sum(jnp.where(same, labels[...].astype(F32), 0.0), axis=1, keepdims=True)
    out[:, :fanout] = ids[...].astype(F32) + label * nodes
    out[:, fanout:] = wts[...]
    into[3].wait()


def load_kernel(after, *refs):
    del after
    count = len(refs) // 2
    for c in launch(refs[-1], tuple(zip(refs[:count], refs[count:-1]))):
        c.wait()


def own_kernel(x, w1, w2, w3, after, scores):
    del after
    hidden = activate(nn(x[...], w1[...]))[0]
    hidden = activate(nn(hidden, w2[...]))[0]
    scores[...] = nt(w3[...], hidden).astype(BF)


def layers(x, w1, w2, xt, h1t, h2, s1, s2, one, two):
    cols = pl.ds(device_slice(), LANE)
    rows = x[...]
    xt[...] = rows.T
    hidden, slope = activate(nn(rows, w1[...]))
    h1t[...] = hidden.T
    one[...] = slope
    s1[...] = one[:, cols]
    hidden, slope = activate(nn(hidden, w2[...]))
    two[...] = hidden
    s2[...] = slope
    h2[...] = two[:, cols]


def again_kernel(x, w1, w2, after, xt, h1t, h2, s1, s2, one, two):
    del after
    layers(x, w1, w2, xt, h1t, h2, s1, s2, one, two)


def peer_kernel(mine, theirs, w1, w2, xt, h1t, h2, s1, s2, x, one, two):
    half = mine.shape[0]
    core = lax.axis_index("batch")
    x[pl.ds(pl.multiple_of(core * half, half), half), :] = mine[...]
    x[pl.ds(pl.multiple_of((1 - core) * half, half), half), :] = theirs[...]
    layers(x, w1, w2, xt, h1t, h2, s1, s2, one, two)


def spread(nodes, packed, high, low, label, ids, wts):
    fanout = ids.shape[0]
    targets = ids.shape[1]
    rows = packed.shape[0]
    node_dev = high.shape[0] // 2
    p = packed[...]
    if rows < LANE:
        p = jnp.concatenate([p] * (LANE // rows), axis=0)
    t = p.T
    parts = [t[i * fanout : (i + 1) * fanout] for i in range(4)]
    if rows < LANE:
        lane = lax.broadcasted_iota(jnp.int32, (fanout, LANE), 1)
        coded = jnp.where(lane < rows, parts[0], parts[2])
        wts[...] = jnp.where(lane < rows, parts[1], parts[3])
    else:
        coded = jnp.concatenate([parts[0], parts[2]], axis=1)
        wts[...] = jnp.concatenate([parts[1], parts[3]], axis=1)
    cls = jnp.floor(coded * (1.0 / nodes))
    label[...] = cls[0:1].astype(jnp.int32)
    ids[...] = (coded - cls * nodes).astype(jnp.int32)
    me = lax.axis_index("owner")
    block = 64
    per_side = node_dev // block

    def step(i, carry):
        side = i // per_side
        owner = jnp.where(side == 0, me, me + 1 - 2 * lax.rem(me, 2))
        base = owner * node_dev + lax.rem(i, per_side) * block
        node = lax.broadcasted_iota(jnp.int32, (block, LANE), 0) + base
        at = pl.ds(pl.multiple_of(i * block, block), block)
        for c in range(targets // LANE):
            cols = slice(c * LANE, (c + 1) * LANE)
            total = jnp.zeros((block, LANE), F32)
            for k in range(fanout):
                total += jnp.where(ids[k : k + 1, cols] == node, wts[k : k + 1, cols], 0.0)
            top, rest = split(total)
            high[at, cols] = top
            low[at, cols] = rest
        return carry

    lax.fori_loop(0, 2 * per_side, step, 0)


def logit_kernel(mine, theirs, high, low, part, send):
    n = mine.shape[1]
    total = nn(mine[...], high[:n]) + nn(mine[...], low[:n])
    total += nn(theirs[...], high[n:]) + nn(theirs[...], low[n:])
    part[...] = total
    send[...] = total.astype(BF)


def spread_kernel(nodes, packed, high, low, label, ids, wts):
    spread(nodes, packed, high, low, label, ids, wts)


def softmax_kernel(logits, got, label, grad, send, loss):
    v = logits[...] + got[...].astype(F32)
    top = jnp.max(v, axis=0, keepdims=True)
    e = jnp.exp(v - top)
    total = jnp.sum(e, axis=0, keepdims=True)
    hit = lax.broadcasted_iota(jnp.int32, v.shape, 0) == label[...]
    loss[...] = jnp.log(total) + top - jnp.sum(jnp.where(hit, v, 0.0), axis=0, keepdims=True)
    g = e / total - jnp.where(hit, 1.0, 0.0)
    grad[...] = g
    send[...] = g.astype(BF)


def back_kernel(bit, grad, far_grad, high, low, far_high, far_low, xt, pxt, h1t, ph1t, h2, ph2, s1, ps1, s2, ps2, w3t, w2, send, keep, acc, two):
    top, rest = split(grad[...])
    far = far_grad[...]
    depth, n = xt.shape
    hidden = h1t.shape[0]
    classes = w3t.shape[0]
    cols = pl.ds(device_slice(), LANE)
    w2_rows = w2[cols, :]
    sides = (slice(0, n), slice(n, 2 * n))
    left = [jnp.concatenate([high[at], low[at], high[at], far_high[at], far_low[at]], axis=1) for at in sides]
    right = jnp.concatenate([top, top, rest, far, far], axis=1)
    g = [nt(v, right).astype(BF) for v in left]
    b2 = [(nn(v, w3t[...]) * s[...]).astype(BF) for v, s in zip(g, (s2, ps2))]
    two[0] = b2[0]
    two[1] = b2[1]
    b1 = [(nt(v, w2_rows) * s[...]).astype(BF) for v, s in zip(b2, (s1, ps1))]
    gt = [nt(right, v).astype(BF) for v in left]
    acc[depth + hidden : depth + hidden + classes] = nn(gt[0], h2[...]) + nn(gt[1], ph2[...])
    acc[depth : depth + hidden] = nn(h1t[...], two[0, :, cols]) + nn(ph1t[...], two[1, :, cols])
    acc[:depth] = nn(xt[...], b1[0]) + nn(pxt[...], b1[1])
    blank = acc.shape[0] - (depth + hidden + classes)
    if blank:
        acc[depth + hidden + classes :] = jnp.zeros((blank, LANE), F32)
    halve(bit, acc, send, keep)


def halve(bit, acc, send, keep):
    rows = acc.shape[0] // 2
    up = lax.rem(lax.axis_index("owner") // bit, 2)
    send[...] = acc[pl.ds(pl.multiple_of((1 - up) * rows, 8), rows), :].astype(BF)
    keep[...] = acc[pl.ds(pl.multiple_of(up * rows, 8), rows), :]


def add_kernel(bit, kept, got, send, keep, acc):
    acc[...] = kept[...] + got[...].astype(F32)
    halve(bit, acc, send, keep)


def sum_kernel(kept, got, out):
    out[...] = (kept[...].astype(F32) + got[...].astype(F32)).astype(BF)


def join_kernel(bit, mine, got, out):
    rows = mine.shape[0]
    up = lax.rem(lax.axis_index("owner") // bit, 2)
    out[pl.ds(pl.multiple_of(up * rows, ROW), rows), :] = mine[...]
    out[pl.ds(pl.multiple_of((1 - up) * rows, ROW), rows), :] = got[...]


def fill(order, halves, sides, outs):
    rows = halves[0].shape[0]
    for i, (s, h) in enumerate(sides):
        cols = pl.ds(pl.multiple_of((2 * s + h) * LANE, LANE), LANE)
        for j in range(2):
            ref = halves[2 * i + order[j]]
            if ref is None:
                continue
            top = 0
            for out in outs:
                low, high = max(top, j * rows), min(top + out.shape[0], (j + 1) * rows)
                if low < high:
                    out[low - top : high - top, cols] = ref[low - j * rows : high - j * rows]
                top += out.shape[0]


def place_kernel(bit, *refs):
    halves, outs = refs[:8], refs[8:]
    me = lax.axis_index("owner")
    side = lax.rem(me, 2)
    core = lax.axis_index("batch")
    up = lax.rem(me // bit, 2)
    sides = ((side, core), (1 - side, core), (side, 1 - core), (1 - side, 1 - core))

    @pl.when(up == 0)
    def _():
        fill((0, 1), halves, sides, outs)

    @pl.when(up == 1)
    def _():
        fill((1, 0), halves, sides, outs)


def whole(kernel, outs, scratch, *args, flops=1000000, limit=24, far_in=(), far_out=()):
    def spec(i, far):
        return pl.BlockSpec(memory_space=pltpu.HBM if i in far else pltpu.VMEM)

    args = [
        pltpu.with_memory_space_constraint(x, pltpu.HBM) if i in far_in else x for i, x in enumerate(args)
    ]
    return pl.pallas_call(
        kernel,
        out_shape=[jax.ShapeDtypeStruct(shape, kind) for shape, kind in outs],
        in_specs=[spec(i, far_in) for i in range(len(args))],
        out_specs=[spec(i, far_out) for i in range(len(outs))],
        scratch_shapes=[
            pltpu.SemaphoreType.DMA((s,)) if isinstance(s, int) else pltpu.VMEM(*s) for s in scratch
        ],
        compiler_params=pltpu.CompilerParams(vmem_limit_bytes=limit << 20),
        cost_estimate=pl.CostEstimate(flops=flops, bytes_accessed=flops // 512, transcendentals=0),
    )(*args)


def body(features, w_first, w_second, w_third, nbr_ids, nbr_weight, labels):
    owners = lax.axis_size("owner")
    node_dev, depth = features.shape
    hidden, classes = w_third.shape
    rows, fanout = nbr_ids.shape
    nodes = owners * node_dev
    me = lax.axis_index("owner")
    core = lax.axis_index("batch")
    bits = [1 << i for i in range(1, owners.bit_length() - 1)]
    targets = owners * rows

    def over(x, bit):
        return lax.ppermute(x, "owner", [(i, i ^ bit) for i in range(owners)])

    def other_core(x):
        return lax.ppermute(x, "batch", [(0, 1), (1, 0)])

    w3t = w_third.T
    half = node_dev // 2
    w1_type, w2_type, x_type = (w_first.shape, BF), (w_second.shape, BF), (features.shape, BF)
    packed, my_half = whole(
        functools.partial(pack_kernel, nodes),
        [((rows, 2 * fanout), F32), ((half, depth), BF)],
        [((rows, fanout), jnp.int32), ((rows, fanout), F32), ((1, rows), jnp.int32), 4],
        nbr_ids,
        nbr_weight,
        labels.reshape(1, rows),
        features,
        limit=PACK,
        far_in=range(4),
    )
    peer_half = over(my_half, 1)
    got = other_core(packed)
    packed = jnp.where(core == 0, jnp.concatenate([packed, got], 1), jnp.concatenate([got, packed], 1))
    features, w_first, w_second, w3t = whole(
        load_kernel,
        [x_type, w1_type, w2_type, (w3t.shape, BF)],
        [4],
        packed,
        features,
        w_first,
        w_second,
        w3t,
        limit=PACK,
        far_in=range(1, 5),
    )
    (scores,) = whole(
        own_kernel,
        [((classes, node_dev), BF)],
        [],
        features,
        w_first,
        w_second,
        w3t,
        packed,
        flops=2000000000,
        limit=16,
    )
    for bit in bits:
        got = over(packed, bit)
        if bit == bits[0]:
            got, scores = lax.optimization_barrier((got, scores))
        up = (me // bit) % 2
        packed = jnp.where(up == 0, jnp.concatenate([packed, got], 0), jnp.concatenate([got, packed], 0))
    far_scores = over(scores, 1)

    big = 24 if owners <= 8 else 48
    maps = [((2 * node_dev, targets), BF), ((2 * node_dev, targets), BF), ((1, targets), jnp.int32)]
    tables = [((fanout, targets), jnp.int32), ((fanout, targets), F32)]
    spread_call = functools.partial(whole, functools.partial(spread_kernel, nodes), maps, tables, limit=big, flops=1000000000)
    high, low, label = spread_call(packed)
    part, send = whole(
        logit_kernel,
        [((classes, targets), F32), ((classes, targets), BF)],
        [],
        scores,
        far_scores,
        high,
        low,
        limit=big,
    )
    kept = [
        ((depth, node_dev), BF),
        ((hidden, node_dev), BF),
        ((node_dev, LANE), BF),
        ((node_dev, LANE), F32),
        ((node_dev, hidden), F32),
    ]
    work = [((node_dev, hidden), F32), ((node_dev, hidden), BF)]
    packed = lax.optimization_barrier((packed, send))[0]
    far_packed = over(packed, 1)
    peer_half = lax.optimization_barrier((peer_half, send))[0]
    peer_rest = other_core(peer_half)
    xt, h1t, h2, s1, s2 = whole(
        again_kernel, kept, work, features, w_first, w_second, send, flops=2000000000
    )
    for bit in bits[:-1]:
        got = over(send, bit)
        if bit == bits[0]:
            got = lax.optimization_barrier((got, s1))[0]
        part = part + got.astype(F32)
        send = part.astype(BF)
    far_packed = lax.optimization_barrier((far_packed, send))[0]
    far_high, far_low, _ = spread_call(far_packed)
    got = over(send, bits[-1])
    peer_rest = lax.optimization_barrier((peer_rest, got))[0]
    pxt, ph1t, ph2, ps1, ps2 = whole(
        peer_kernel,
        kept,
        [x_type] + work,
        peer_half,
        peer_rest,
        w_first,
        w_second,
        flops=2000000000,
    )
    got = lax.optimization_barrier((got, far_high))[0]
    grad, grad_send, loss = whole(
        softmax_kernel,
        [((classes, targets), F32), ((classes, targets), BF), ((1, targets), F32)],
        [],
        part,
        got,
        label,
    )
    at = core * (targets // 2) + (me // 2) * rows
    target_loss = lax.dynamic_slice_in_dim(loss[0], at, rows, 0)
    far_grad = over(grad_send, 1)

    step = ROW << (len(bits) - 1)
    stack = -(-(depth + hidden + classes) // step) * step

    def halves(n):
        return [((n // 2, LANE), BF), ((n // 2, LANE), F32)]

    send, keep = whole(
        functools.partial(back_kernel, bits[0]),
        halves(stack),
        [((stack, LANE), F32), ((2, node_dev, hidden), BF)],
        grad, far_grad, high, low, far_high, far_low,
        xt, pxt, h1t, ph1t, h2, ph2, s1, ps1, s2, ps2, w3t, w_second,
        limit=big,
    )
    size = stack // 2
    for at, bit in enumerate(bits[1:-1]):
        send, keep = whole(
            functools.partial(add_kernel, bit),
            halves(size),
            [((size, LANE), F32)],
            keep,
            over(send, bits[at]),
        )
        size //= 2
    for mine, bit in ((keep, bits[-2]), (None, bits[-1])):
        got = over(send, bit)
        (send,) = whole(sum_kernel, [((size, LANE), BF)], [], send if mine is None else mine, got)
    out = send
    for bit in reversed(bits[1:-1]):
        size *= 2
        (out,) = whole(functools.partial(join_kernel, bit), [((size, LANE), BF)], [], out, over(out, bit))
    pair = (out, over(out, bits[0]))
    across = [over(p, 1) for p in pair]
    cores = [other_core(p) for p in pair]
    both = [other_core(p) for p in across]
    first, second, third = whole(
        functools.partial(place_kernel, bits[0]),
        [((depth, hidden), BF), ((hidden, hidden), BF), ((classes, hidden), BF)],
        [],
        *pair,
        *across,
        *cores,
        *both,
    )
    return first, second, third.T, target_loss


def solution(mesh):
    in_specs = (
        P("owner", None),
        P(),
        P(),
        P(),
        P(("groups", "owner", "batch"), None),
        P(("groups", "owner", "batch"), None),
        P(("groups", "owner", "batch")),
    )
    out_specs = (
        P("groups", None),
        P("groups", None),
        P("groups", None),
        P(("groups", "owner", "batch")),
    )
    return jax.shard_map(body, mesh=mesh, in_specs=in_specs, out_specs=out_specs, check_vma=False)
```

```python
import functools
import jax
import jax.numpy as jnp
from jax import lax
from jax.experimental import pallas as pl
from jax.experimental.pallas import tpu as pltpu
from jax.sharding import PartitionSpec as P

BF = jnp.bfloat16
F32 = jnp.float32
ROW = 16
LANE = 128
PACK = 16


def nn(a, b):
    return lax.dot_general(a, b, (((1,), (0,)), ((), ())), preferred_element_type=F32)


def nt(a, b):
    return lax.dot_general(a, b, (((1,), (1,)), ((), ())), preferred_element_type=F32)


def split(v):
    high = v.astype(BF)
    return high, (v - high.astype(F32)).astype(BF)


def device_slice():
    place = lax.rem(lax.axis_index("owner"), 2) * 2 + lax.axis_index("batch")
    return pl.multiple_of(place * LANE, LANE)


def activate(pre):
    sigma = 0.5 * jnp.tanh(0.5 * pre) + 0.5
    return (pre * sigma).astype(BF), sigma * (1.0 + pre * (1.0 - sigma))


def launch(sem, pairs):
    copies = [pltpu.make_async_copy(a, b, sem.at[i]) for i, (a, b) in enumerate(pairs)]
    for c in copies:
        c.start()
    return copies


def pack_kernel(nodes, ids_hbm, wts_hbm, labels_hbm, x_hbm, out, near, late, ids, wts, labels, sem):
    rows, fanout = ids.shape
    start = lax.axis_index("batch") * (x_hbm.shape[0] // 2)
    pairs = ((labels_hbm, labels), (ids_hbm, ids), (wts_hbm, wts))
    for piece in (near, late):
        pairs += ((x_hbm.at[pl.ds(pl.multiple_of(start, ROW), piece.shape[0]), :], piece),)
        start = start + piece.shape[0]
    into = launch(sem, pairs)
    for c in into[:3]:
        c.wait()
    shape = (rows, rows)
    same = lax.broadcasted_iota(jnp.int32, shape, 0) == lax.broadcasted_iota(jnp.int32, shape, 1)
    label = jnp.sum(jnp.where(same, labels[...].astype(F32), 0.0), axis=1, keepdims=True)
    out[:, :fanout] = ids[...].astype(F32) + label * nodes
    out[:, fanout:] = wts[...]
    into[3].wait()
    into[4].wait()


def load_kernel(after, *refs):
    del after
    count = len(refs) // 2
    for c in launch(refs[-1], tuple(zip(refs[:count], refs[count:-1]))):
        c.wait()


def own_kernel(x, w1, w2, w3, after, scores):
    del after
    hidden = activate(nn(x[...], w1[...]))[0]
    hidden = activate(nn(hidden, w2[...]))[0]
    scores[...] = nt(w3[...], hidden).astype(BF)


def layers(x, w1, w2, xt, h1t, h2, s1, s2, one, two):
    cols = pl.ds(device_slice(), LANE)
    rows = x[...]
    xt[...] = rows.T
    hidden, slope = activate(nn(rows, w1[...]))
    h1t[...] = hidden.T
    one[...] = slope
    s1[...] = one[:, cols]
    hidden, slope = activate(nn(hidden, w2[...]))
    two[...] = hidden
    s2[...] = slope
    h2[...] = two[:, cols]


def again_kernel(x, w1, w2, after, xt, h1t, h2, s1, s2, one, two):
    del after
    layers(x, w1, w2, xt, h1t, h2, s1, s2, one, two)


def peer_kernel(near, late, far_near, far_late, w1, w2, xt, h1t, h2, s1, s2, x, one, two):
    core = lax.axis_index("batch")
    for side, pieces in ((core, (near, late)), (1 - core, (far_near, far_late))):
        start = side * (x.shape[0] // 2)
        for piece in pieces:
            x[pl.ds(pl.multiple_of(start, ROW), piece.shape[0]), :] = piece[...]
            start = start + piece.shape[0]
    layers(x, w1, w2, xt, h1t, h2, s1, s2, one, two)


def spread(nodes, packed, high, low, label, ids, wts):
    fanout = ids.shape[0]
    targets = ids.shape[1]
    rows = packed.shape[0]
    node_dev = high.shape[0] // 2
    p = packed[...]
    if rows < LANE:
        p = jnp.concatenate([p] * (LANE // rows), axis=0)
    t = p.T
    parts = [t[i * fanout : (i + 1) * fanout] for i in range(4)]
    if rows < LANE:
        lane = lax.broadcasted_iota(jnp.int32, (fanout, LANE), 1)
        coded = jnp.where(lane < rows, parts[0], parts[2])
        wts[...] = jnp.where(lane < rows, parts[1], parts[3])
    else:
        coded = jnp.concatenate([parts[0], parts[2]], axis=1)
        wts[...] = jnp.concatenate([parts[1], parts[3]], axis=1)
    cls = jnp.floor(coded * (1.0 / nodes))
    label[...] = cls[0:1].astype(jnp.int32)
    ids[...] = (coded - cls * nodes).astype(jnp.int32)
    me = lax.axis_index("owner")
    block = 64
    per_side = node_dev // block

    def step(i, carry):
        side = i // per_side
        owner = jnp.where(side == 0, me, me + 1 - 2 * lax.rem(me, 2))
        base = owner * node_dev + lax.rem(i, per_side) * block
        node = lax.broadcasted_iota(jnp.int32, (block, LANE), 0) + base
        at = pl.ds(pl.multiple_of(i * block, block), block)
        for c in range(targets // LANE):
            cols = slice(c * LANE, (c + 1) * LANE)
            total = jnp.zeros((block, LANE), F32)
            for k in range(fanout):
                total += jnp.where(ids[k : k + 1, cols] == node, wts[k : k + 1, cols], 0.0)
            top, rest = split(total)
            high[at, cols] = top
            low[at, cols] = rest
        return carry

    lax.fori_loop(0, 2 * per_side, step, 0)


def logit_kernel(mine, theirs, high, low, part, send):
    n = mine.shape[1]
    total = nn(mine[...], high[:n]) + nn(mine[...], low[:n])
    total += nn(theirs[...], high[n:]) + nn(theirs[...], low[n:])
    part[...] = total
    send[...] = total.astype(BF)


def spread_kernel(nodes, packed, high, low, label, ids, wts):
    spread(nodes, packed, high, low, label, ids, wts)


def softmax_kernel(logits, got, label, grad, send, loss):
    v = logits[...] + got[...].astype(F32)
    top = jnp.max(v, axis=0, keepdims=True)
    e = jnp.exp(v - top)
    total = jnp.sum(e, axis=0, keepdims=True)
    hit = lax.broadcasted_iota(jnp.int32, v.shape, 0) == label[...]
    loss[...] = jnp.log(total) + top - jnp.sum(jnp.where(hit, v, 0.0), axis=0, keepdims=True)
    g = e / total - jnp.where(hit, 1.0, 0.0)
    grad[...] = g
    send[...] = g.astype(BF)


def back_kernel(bit, grad, far_grad, high, low, far_high, far_low, xt, pxt, h1t, ph1t, h2, ph2, s1, ps1, s2, ps2, w3t, w2, send, keep, acc, two):
    top, rest = split(grad[...])
    far = far_grad[...]
    depth, n = xt.shape
    hidden = h1t.shape[0]
    classes = w3t.shape[0]
    cols = pl.ds(device_slice(), LANE)
    w2_rows = w2[cols, :]
    sides = (slice(0, n), slice(n, 2 * n))
    left = [jnp.concatenate([high[at], low[at], high[at], far_high[at], far_low[at]], axis=1) for at in sides]
    right = jnp.concatenate([top, top, rest, far, far], axis=1)
    g = [nt(v, right).astype(BF) for v in left]
    b2 = [(nn(v, w3t[...]) * s[...]).astype(BF) for v, s in zip(g, (s2, ps2))]
    two[0] = b2[0]
    two[1] = b2[1]
    b1 = [(nt(v, w2_rows) * s[...]).astype(BF) for v, s in zip(b2, (s1, ps1))]
    gt = [nt(right, v).astype(BF) for v in left]
    acc[depth + hidden : depth + hidden + classes] = nn(gt[0], h2[...]) + nn(gt[1], ph2[...])
    acc[depth : depth + hidden] = nn(h1t[...], two[0, :, cols]) + nn(ph1t[...], two[1, :, cols])
    acc[:depth] = nn(xt[...], b1[0]) + nn(pxt[...], b1[1])
    blank = acc.shape[0] - (depth + hidden + classes)
    if blank:
        acc[depth + hidden + classes :] = jnp.zeros((blank, LANE), F32)
    halve(bit, acc, send, keep)


def halve(bit, acc, send, keep):
    rows = acc.shape[0] // 2
    up = lax.rem(lax.axis_index("owner") // bit, 2)
    send[...] = acc[pl.ds(pl.multiple_of((1 - up) * rows, 8), rows), :].astype(BF)
    keep[...] = acc[pl.ds(pl.multiple_of(up * rows, 8), rows), :]


def add_kernel(bit, kept, got, send, keep, acc):
    acc[...] = kept[...] + got[...].astype(F32)
    halve(bit, acc, send, keep)


def sum_kernel(kept, got, out):
    out[...] = (kept[...].astype(F32) + got[...].astype(F32)).astype(BF)


def join_kernel(bit, mine, got, out):
    rows = mine.shape[0]
    up = lax.rem(lax.axis_index("owner") // bit, 2)
    out[pl.ds(pl.multiple_of(up * rows, ROW), rows), :] = mine[...]
    out[pl.ds(pl.multiple_of((1 - up) * rows, ROW), rows), :] = got[...]


def fill(order, halves, sides, outs):
    rows = halves[0].shape[0]
    for i, (s, h) in enumerate(sides):
        cols = pl.ds(pl.multiple_of((2 * s + h) * LANE, LANE), LANE)
        for j in range(2):
            ref = halves[2 * i + order[j]]
            if ref is None:
                continue
            top = 0
            for out in outs:
                low, high = max(top, j * rows), min(top + out.shape[0], (j + 1) * rows)
                if low < high:
                    out[low - top : high - top, cols] = ref[low - j * rows : high - j * rows]
                top += out.shape[0]


def place_kernel(bit, *refs):
    halves, outs = refs[:8], refs[8:]
    me = lax.axis_index("owner")
    side = lax.rem(me, 2)
    core = lax.axis_index("batch")
    up = lax.rem(me // bit, 2)
    sides = ((side, core), (1 - side, core), (side, 1 - core), (1 - side, 1 - core))

    @pl.when(up == 0)
    def _():
        fill((0, 1), halves, sides, outs)

    @pl.when(up == 1)
    def _():
        fill((1, 0), halves, sides, outs)


def whole(kernel, outs, scratch, *args, flops=1000000, limit=24, far_in=(), far_out=()):
    def spec(i, far):
        return pl.BlockSpec(memory_space=pltpu.HBM if i in far else pltpu.VMEM)

    args = [
        pltpu.with_memory_space_constraint(x, pltpu.HBM) if i in far_in else x for i, x in enumerate(args)
    ]
    return pl.pallas_call(
        kernel,
        out_shape=[jax.ShapeDtypeStruct(shape, kind) for shape, kind in outs],
        in_specs=[spec(i, far_in) for i in range(len(args))],
        out_specs=[spec(i, far_out) for i in range(len(outs))],
        scratch_shapes=[
            pltpu.SemaphoreType.DMA((s,)) if isinstance(s, int) else pltpu.VMEM(*s) for s in scratch
        ],
        compiler_params=pltpu.CompilerParams(vmem_limit_bytes=limit << 20),
        cost_estimate=pl.CostEstimate(flops=flops, bytes_accessed=flops // 512, transcendentals=0),
    )(*args)


def body(features, w_first, w_second, w_third, nbr_ids, nbr_weight, labels):
    owners = lax.axis_size("owner")
    node_dev, depth = features.shape
    hidden, classes = w_third.shape
    rows, fanout = nbr_ids.shape
    nodes = owners * node_dev
    me = lax.axis_index("owner")
    core = lax.axis_index("batch")
    bits = [1 << i for i in range(1, owners.bit_length() - 1)]
    targets = owners * rows

    def over(x, bit):
        return lax.ppermute(x, "owner", [(i, i ^ bit) for i in range(owners)])

    def other_core(x):
        return lax.ppermute(x, "batch", [(0, 1), (1, 0)])

    w3t = w_third.T
    near = 5 * node_dev // 16
    w1_type, w2_type, x_type = (w_first.shape, BF), (w_second.shape, BF), (features.shape, BF)
    packed, my_near, my_late = whole(
        functools.partial(pack_kernel, nodes),
        [((rows, 2 * fanout), F32), ((near, depth), BF), ((node_dev // 2 - near, depth), BF)],
        [((rows, fanout), jnp.int32), ((rows, fanout), F32), ((1, rows), jnp.int32), 5],
        nbr_ids,
        nbr_weight,
        labels.reshape(1, rows),
        features,
        limit=PACK,
        far_in=range(4),
    )
    peer_near = over(my_near, 1)
    got = other_core(packed)
    packed = jnp.where(core == 0, jnp.concatenate([packed, got], 1), jnp.concatenate([got, packed], 1))
    features, w_first, w_second, w3t = whole(
        load_kernel,
        [x_type, w1_type, w2_type, (w3t.shape, BF)],
        [4],
        packed,
        features,
        w_first,
        w_second,
        w3t,
        limit=PACK,
        far_in=range(1, 5),
    )
    (scores,) = whole(
        own_kernel,
        [((classes, node_dev), BF)],
        [],
        features,
        w_first,
        w_second,
        w3t,
        packed,
        flops=1000,
        limit=16,
    )
    for bit in bits:
        got = over(packed, bit)
        if bit == bits[0]:
            got, scores = lax.optimization_barrier((got, scores))
        if bit == bits[-1]:
            got, peer_near = lax.optimization_barrier((got, peer_near))
        up = (me // bit) % 2
        packed = jnp.where(up == 0, jnp.concatenate([packed, got], 0), jnp.concatenate([got, packed], 0))
    far_scores = over(scores, 1)

    big = 24 if owners <= 8 else 48
    maps = [((2 * node_dev, targets), BF), ((2 * node_dev, targets), BF), ((1, targets), jnp.int32)]
    tables = [((fanout, targets), jnp.int32), ((fanout, targets), F32)]
    spread_call = functools.partial(whole, functools.partial(spread_kernel, nodes), maps, tables, limit=big, flops=1000000000)
    high, low, label = spread_call(packed)
    my_late = lax.optimization_barrier((my_late, high))[0]
    peer_late = over(my_late, 1)
    part, send = whole(
        logit_kernel,
        [((classes, targets), F32), ((classes, targets), BF)],
        [],
        scores,
        far_scores,
        high,
        low,
        limit=big,
    )
    kept = [
        ((depth, node_dev), BF),
        ((hidden, node_dev), BF),
        ((node_dev, LANE), BF),
        ((node_dev, LANE), F32),
        ((node_dev, hidden), F32),
    ]
    work = [((node_dev, hidden), F32), ((node_dev, hidden), BF)]
    packed = lax.optimization_barrier((packed, send))[0]
    far_packed = over(packed, 1)
    xt, h1t, h2, s1, s2 = whole(
        again_kernel, kept, work, features, w_first, w_second, send, flops=1000
    )
    peer_near, peer_late = lax.optimization_barrier((peer_near, peer_late, s1))[:2]
    far_near, far_late = other_core(peer_near), other_core(peer_late)
    for bit in bits[:-1]:
        got = over(send, bit)
        if bit == bits[0]:
            got = lax.optimization_barrier((got, s1))[0]
        part = part + got.astype(F32)
        send = part.astype(BF)
    far_packed = lax.optimization_barrier((far_packed, send))[0]
    far_high, far_low, _ = spread_call(far_packed)
    got = over(send, bits[-1])
    got = lax.optimization_barrier((got, far_high))[0]
    grad, grad_send, loss = whole(
        softmax_kernel,
        [((classes, targets), F32), ((classes, targets), BF), ((1, targets), F32)],
        [],
        part,
        got,
        label,
    )
    at = core * (targets // 2) + (me // 2) * rows
    target_loss = lax.dynamic_slice_in_dim(loss[0], at, rows, 0)
    far_grad = over(grad_send, 1)
    far_late = lax.optimization_barrier((far_late, grad_send))[0]
    pxt, ph1t, ph2, ps1, ps2 = whole(
        peer_kernel,
        kept,
        [x_type] + work,
        peer_near,
        peer_late,
        far_near,
        far_late,
        w_first,
        w_second,
        flops=2000000000,
    )

    step = ROW << (len(bits) - 1)
    stack = -(-(depth + hidden + classes) // step) * step

    def halves(n):
        return [((n // 2, LANE), BF), ((n // 2, LANE), F32)]

    send, keep = whole(
        functools.partial(back_kernel, bits[0]),
        halves(stack),
        [((stack, LANE), F32), ((2, node_dev, hidden), BF)],
        grad, far_grad, high, low, far_high, far_low,
        xt, pxt, h1t, ph1t, h2, ph2, s1, ps1, s2, ps2, w3t, w_second,
        limit=big,
    )
    size = stack // 2
    for at, bit in enumerate(bits[1:-1]):
        send, keep = whole(
            functools.partial(add_kernel, bit),
            halves(size),
            [((size, LANE), F32)],
            keep,
            over(send, bits[at]),
        )
        size //= 2
    for mine, bit in ((keep, bits[-2]), (None, bits[-1])):
        got = over(send, bit)
        (send,) = whole(sum_kernel, [((size, LANE), BF)], [], send if mine is None else mine, got)
    out = send
    for bit in reversed(bits[1:-1]):
        size *= 2
        (out,) = whole(functools.partial(join_kernel, bit), [((size, LANE), BF)], [], out, over(out, bit))
    pair = (out, over(out, bits[0]))
    across = [over(p, 1) for p in pair]
    cores = [other_core(p) for p in pair]
    both = [other_core(p) for p in across]
    first, second, third = whole(
        functools.partial(place_kernel, bits[0]),
        [((depth, hidden), BF), ((hidden, hidden), BF), ((classes, hidden), BF)],
        [],
        *pair,
        *across,
        *cores,
        *both,
    )
    return first, second, third.T, target_loss


def solution(mesh):
    in_specs = (
        P("owner", None),
        P(),
        P(),
        P(),
        P(("groups", "owner", "batch"), None),
        P(("groups", "owner", "batch"), None),
        P(("groups", "owner", "batch")),
    )
    out_specs = (
        P("groups", None),
        P("groups", None),
        P("groups", None),
        P(("groups", "owner", "batch")),
    )
    return jax.shard_map(body, mesh=mesh, in_specs=in_specs, out_specs=out_specs, check_vma=False)
```

```python
import functools
import jax
import jax.numpy as jnp
from jax import lax
from jax.experimental import pallas as pl
from jax.experimental.pallas import tpu as pltpu
from jax.sharding import PartitionSpec as P

BF = jnp.bfloat16
F32 = jnp.float32
ROW = 16
LANE = 128
PACK = 16


def nn(a, b):
    return lax.dot_general(a, b, (((1,), (0,)), ((), ())), preferred_element_type=F32)


def nt(a, b):
    return lax.dot_general(a, b, (((1,), (1,)), ((), ())), preferred_element_type=F32)


def tn(a, b):
    return lax.dot_general(a, b, (((0,), (0,)), ((), ())), preferred_element_type=F32)


def split(v):
    high = v.astype(BF)
    return high, (v - high.astype(F32)).astype(BF)


def device_slice():
    place = lax.rem(lax.axis_index("owner"), 2) * 2 + lax.axis_index("batch")
    return pl.multiple_of(place * LANE, LANE)


def activate(pre):
    sigma = 0.5 * jnp.tanh(0.5 * pre) + 0.5
    return (pre * sigma).astype(BF), sigma * (1.0 + pre * (1.0 - sigma))


def launch(sem, pairs):
    copies = [pltpu.make_async_copy(a, b, sem.at[i]) for i, (a, b) in enumerate(pairs)]
    for c in copies:
        c.start()
    return copies


def pack_kernel(nodes, ids_hbm, wts_hbm, labels_hbm, x_hbm, out, near, late, ids, wts, labels, sem):
    rows, fanout = ids.shape
    start = lax.axis_index("batch") * (x_hbm.shape[0] // 2)
    pairs = ((labels_hbm, labels), (ids_hbm, ids), (wts_hbm, wts))
    for piece in (near, late):
        pairs += ((x_hbm.at[pl.ds(pl.multiple_of(start, ROW), piece.shape[0]), :], piece),)
        start = start + piece.shape[0]
    into = launch(sem, pairs)
    for c in into[:3]:
        c.wait()
    shape = (rows, rows)
    same = lax.broadcasted_iota(jnp.int32, shape, 0) == lax.broadcasted_iota(jnp.int32, shape, 1)
    label = jnp.sum(jnp.where(same, labels[...].astype(F32), 0.0), axis=1, keepdims=True)
    out[:, :fanout] = ids[...].astype(F32) + label * nodes
    out[:, fanout:] = wts[...]
    into[3].wait()
    into[4].wait()


def load_kernel(after, *refs):
    del after
    count = len(refs) // 2
    for c in launch(refs[-1], tuple(zip(refs[:count], refs[count:-1]))):
        c.wait()


def own_kernel(x, w1, w2, w3, after, scores):
    del after
    hidden = activate(nn(x[...], w1[...]))[0]
    hidden = activate(nn(hidden, w2[...]))[0]
    scores[...] = nt(w3[...], hidden).astype(BF)


def layers(x, w1, w2, xt, h1t, h2, s1, s2, one, two):
    cols = pl.ds(device_slice(), LANE)
    rows = x[...]
    xt[...] = rows.T
    hidden, slope = activate(nn(rows, w1[...]))
    h1t[...] = hidden.T
    one[...] = slope
    s1[...] = one[:, cols]
    hidden, slope = activate(nn(hidden, w2[...]))
    two[...] = hidden
    s2[...] = slope
    h2[...] = two[:, cols]


def again_kernel(x, w1, w2, after, xt, h1t, h2, s1, s2, one, two):
    del after
    layers(x, w1, w2, xt, h1t, h2, s1, s2, one, two)


def peer_kernel(near, late, far_near, far_late, w1, w2, xt, h1t, h2, s1, s2, x, one, two):
    core = lax.axis_index("batch")
    for side, pieces in ((core, (near, late)), (1 - core, (far_near, far_late))):
        start = side * (x.shape[0] // 2)
        for piece in pieces:
            x[pl.ds(pl.multiple_of(start, ROW), piece.shape[0]), :] = piece[...]
            start = start + piece.shape[0]
    layers(x, w1, w2, xt, h1t, h2, s1, s2, one, two)


def spread(nodes, packed, high, low, label, ids, wts):
    fanout = ids.shape[0]
    targets = ids.shape[1]
    rows = packed.shape[0]
    node_dev = high.shape[0] // 2
    p = packed[...]
    if rows < LANE:
        p = jnp.concatenate([p] * (LANE // rows), axis=0)
    t = p.T
    parts = [t[i * fanout : (i + 1) * fanout] for i in range(4)]
    if rows < LANE:
        lane = lax.broadcasted_iota(jnp.int32, (fanout, LANE), 1)
        coded = jnp.where(lane < rows, parts[0], parts[2])
        wts[...] = jnp.where(lane < rows, parts[1], parts[3])
    else:
        coded = jnp.concatenate([parts[0], parts[2]], axis=1)
        wts[...] = jnp.concatenate([parts[1], parts[3]], axis=1)
    cls = jnp.floor(coded * (1.0 / nodes))
    label[...] = cls[0:1].astype(jnp.int32)
    ids[...] = (coded - cls * nodes).astype(jnp.int32)
    me = lax.axis_index("owner")
    block = 64
    per_side = node_dev // block

    def step(i, carry):
        side = i // per_side
        owner = jnp.where(side == 0, me, me + 1 - 2 * lax.rem(me, 2))
        base = owner * node_dev + lax.rem(i, per_side) * block
        node = lax.broadcasted_iota(jnp.int32, (block, LANE), 0) + base
        at = pl.ds(pl.multiple_of(i * block, block), block)
        for c in range(targets // LANE):
            cols = slice(c * LANE, (c + 1) * LANE)
            total = jnp.zeros((block, LANE), F32)
            for k in range(fanout):
                total += jnp.where(ids[k : k + 1, cols] == node, wts[k : k + 1, cols], 0.0)
            top, rest = split(total)
            high[at, cols] = top
            low[at, cols] = rest
        return carry

    lax.fori_loop(0, 2 * per_side, step, 0)


def logit_kernel(mine, theirs, high, low, part, send):
    n = mine.shape[1]
    total = nn(mine[...], high[:n]) + nn(mine[...], low[:n])
    total += nn(theirs[...], high[n:]) + nn(theirs[...], low[n:])
    part[...] = total
    send[...] = total.astype(BF)


def spread_kernel(nodes, packed, high, low, label, ids, wts):
    spread(nodes, packed, high, low, label, ids, wts)


def softmax_kernel(logits, got, label, grad, send, loss):
    v = logits[...] + got[...].astype(F32)
    top = jnp.max(v, axis=0, keepdims=True)
    e = jnp.exp(v - top)
    total = jnp.sum(e, axis=0, keepdims=True)
    hit = lax.broadcasted_iota(jnp.int32, v.shape, 0) == label[...]
    loss[...] = jnp.log(total) + top - jnp.sum(jnp.where(hit, v, 0.0), axis=0, keepdims=True)
    g = e / total - jnp.where(hit, 1.0, 0.0)
    grad[...] = g
    send[...] = g.astype(BF)


def back_kernel(bit, grad, far_grad, high, low, far_high, far_low, xt, pxt, h1t, ph1t, h2, ph2, s1, ps1, s2, ps2, w3t, w2, send, keep, acc, two):
    top, rest = split(grad[...])
    far = far_grad[...]
    depth, n = xt.shape
    hidden = h1t.shape[0]
    classes = w3t.shape[0]
    cols = pl.ds(device_slice(), LANE)
    w2_rows = w2[cols, :]
    sides = (slice(0, n), slice(n, 2 * n))
    own = jnp.concatenate([top, top], axis=1)
    other = jnp.concatenate([rest, far], axis=1)
    g = []
    for at in sides:
        total = nt(jnp.concatenate([high[at], low[at]], axis=1), own)
        total += nt(jnp.concatenate([high[at], far_high[at]], axis=1), other)
        g.append((total + nt(far_low[at], far)).astype(BF))
    b2 = [(nn(v, w3t[...]) * s[...]).astype(BF) for v, s in zip(g, (s2, ps2))]
    two[0] = b2[0]
    two[1] = b2[1]
    b1 = [(nt(v, w2_rows) * s[...]).astype(BF) for v, s in zip(b2, (s1, ps1))]
    acc[depth + hidden : depth + hidden + classes] = tn(g[0], h2[...]) + tn(g[1], ph2[...])
    acc[depth : depth + hidden] = nn(h1t[...], two[0, :, cols]) + nn(ph1t[...], two[1, :, cols])
    acc[:depth] = nn(xt[...], b1[0]) + nn(pxt[...], b1[1])
    blank = acc.shape[0] - (depth + hidden + classes)
    if blank:
        acc[depth + hidden + classes :] = jnp.zeros((blank, LANE), F32)
    halve(bit, acc, send, keep)


def halve(bit, acc, send, keep):
    rows = acc.shape[0] // 2
    up = lax.rem(lax.axis_index("owner") // bit, 2)
    send[...] = acc[pl.ds(pl.multiple_of((1 - up) * rows, 8), rows), :].astype(BF)
    keep[...] = acc[pl.ds(pl.multiple_of(up * rows, 8), rows), :]


def add_kernel(bit, kept, got, send, keep, acc):
    acc[...] = kept[...] + got[...].astype(F32)
    halve(bit, acc, send, keep)


def sum_kernel(kept, got, out):
    out[...] = (kept[...].astype(F32) + got[...].astype(F32)).astype(BF)


def join_kernel(bit, mine, got, out):
    rows = mine.shape[0]
    up = lax.rem(lax.axis_index("owner") // bit, 2)
    out[pl.ds(pl.multiple_of(up * rows, ROW), rows), :] = mine[...]
    out[pl.ds(pl.multiple_of((1 - up) * rows, ROW), rows), :] = got[...]


def fill(order, halves, sides, outs):
    rows = halves[0].shape[0]
    for i, (s, h) in enumerate(sides):
        cols = pl.ds(pl.multiple_of((2 * s + h) * LANE, LANE), LANE)
        for j in range(2):
            ref = halves[2 * i + order[j]]
            if ref is None:
                continue
            top = 0
            for out in outs:
                low, high = max(top, j * rows), min(top + out.shape[0], (j + 1) * rows)
                if low < high:
                    out[low - top : high - top, cols] = ref[low - j * rows : high - j * rows]
                top += out.shape[0]


def place_kernel(bit, *refs):
    halves, outs = refs[:8], refs[8:]
    me = lax.axis_index("owner")
    side = lax.rem(me, 2)
    core = lax.axis_index("batch")
    up = lax.rem(me // bit, 2)
    sides = ((side, core), (1 - side, core), (side, 1 - core), (1 - side, 1 - core))

    @pl.when(up == 0)
    def _():
        fill((0, 1), halves, sides, outs)

    @pl.when(up == 1)
    def _():
        fill((1, 0), halves, sides, outs)


def whole(kernel, outs, scratch, *args, flops=1000000, limit=24, far_in=(), far_out=()):
    def spec(i, far):
        return pl.BlockSpec(memory_space=pltpu.HBM if i in far else pltpu.VMEM)

    args = [
        pltpu.with_memory_space_constraint(x, pltpu.HBM) if i in far_in else x for i, x in enumerate(args)
    ]
    return pl.pallas_call(
        kernel,
        out_shape=[jax.ShapeDtypeStruct(shape, kind) for shape, kind in outs],
        in_specs=[spec(i, far_in) for i in range(len(args))],
        out_specs=[spec(i, far_out) for i in range(len(outs))],
        scratch_shapes=[
            pltpu.SemaphoreType.DMA((s,)) if isinstance(s, int) else pltpu.VMEM(*s) for s in scratch
        ],
        compiler_params=pltpu.CompilerParams(vmem_limit_bytes=limit << 20),
        cost_estimate=pl.CostEstimate(flops=flops, bytes_accessed=flops // 512, transcendentals=0),
    )(*args)


def body(features, w_first, w_second, w_third, nbr_ids, nbr_weight, labels):
    owners = lax.axis_size("owner")
    node_dev, depth = features.shape
    hidden, classes = w_third.shape
    rows, fanout = nbr_ids.shape
    nodes = owners * node_dev
    me = lax.axis_index("owner")
    core = lax.axis_index("batch")
    bits = [1 << i for i in range(1, owners.bit_length() - 1)]
    targets = owners * rows

    def over(x, bit):
        return lax.ppermute(x, "owner", [(i, i ^ bit) for i in range(owners)])

    def other_core(x):
        return lax.ppermute(x, "batch", [(0, 1), (1, 0)])

    w3t = w_third.T
    near = 5 * node_dev // 16
    w1_type, w2_type, x_type = (w_first.shape, BF), (w_second.shape, BF), (features.shape, BF)
    packed, my_near, my_late = whole(
        functools.partial(pack_kernel, nodes),
        [((rows, 2 * fanout), F32), ((near, depth), BF), ((node_dev // 2 - near, depth), BF)],
        [((rows, fanout), jnp.int32), ((rows, fanout), F32), ((1, rows), jnp.int32), 5],
        nbr_ids,
        nbr_weight,
        labels.reshape(1, rows),
        features,
        limit=PACK,
        far_in=range(4),
    )
    peer_near = over(my_near, 1)
    got = other_core(packed)
    packed = jnp.where(core == 0, jnp.concatenate([packed, got], 1), jnp.concatenate([got, packed], 1))
    features, w_first, w_second, w3t = whole(
        load_kernel,
        [x_type, w1_type, w2_type, (w3t.shape, BF)],
        [4],
        packed,
        features,
        w_first,
        w_second,
        w3t,
        limit=PACK,
        far_in=range(1, 5),
    )
    (scores,) = whole(
        own_kernel,
        [((classes, node_dev), BF)],
        [],
        features,
        w_first,
        w_second,
        w3t,
        packed,
        flops=1000,
        limit=16,
    )
    for bit in bits:
        got = over(packed, bit)
        if bit == bits[0]:
            got, scores = lax.optimization_barrier((got, scores))
        if bit == bits[-1]:
            got, peer_near = lax.optimization_barrier((got, peer_near))
        up = (me // bit) % 2
        packed = jnp.where(up == 0, jnp.concatenate([packed, got], 0), jnp.concatenate([got, packed], 0))
    far_scores = over(scores, 1)

    big = 24 if owners <= 8 else 48
    maps = [((2 * node_dev, targets), BF), ((2 * node_dev, targets), BF), ((1, targets), jnp.int32)]
    tables = [((fanout, targets), jnp.int32), ((fanout, targets), F32)]
    spread_call = functools.partial(whole, functools.partial(spread_kernel, nodes), maps, tables, limit=big, flops=1000000000)
    high, low, label = spread_call(packed)
    my_late = lax.optimization_barrier((my_late, high))[0]
    peer_late = over(my_late, 1)
    part, send = whole(
        logit_kernel,
        [((classes, targets), F32), ((classes, targets), BF)],
        [],
        scores,
        far_scores,
        high,
        low,
        limit=big,
    )
    kept = [
        ((depth, node_dev), BF),
        ((hidden, node_dev), BF),
        ((node_dev, LANE), BF),
        ((node_dev, LANE), F32),
        ((node_dev, hidden), F32),
    ]
    work = [((node_dev, hidden), F32), ((node_dev, hidden), BF)]
    packed = lax.optimization_barrier((packed, send))[0]
    far_packed = over(packed, 1)
    xt, h1t, h2, s1, s2 = whole(
        again_kernel, kept, work, features, w_first, w_second, send, flops=1000
    )
    peer_near, peer_late = lax.optimization_barrier((peer_near, peer_late, s1))[:2]
    far_near, far_late = other_core(peer_near), other_core(peer_late)
    for bit in bits[:-1]:
        got = over(send, bit)
        if bit == bits[0]:
            got = lax.optimization_barrier((got, s1))[0]
        part = part + got.astype(F32)
        send = part.astype(BF)
    far_packed = lax.optimization_barrier((far_packed, send))[0]
    far_high, far_low, _ = spread_call(far_packed)
    got = over(send, bits[-1])
    got = lax.optimization_barrier((got, far_high))[0]
    grad, grad_send, loss = whole(
        softmax_kernel,
        [((classes, targets), F32), ((classes, targets), BF), ((1, targets), F32)],
        [],
        part,
        got,
        label,
    )
    at = core * (targets // 2) + (me // 2) * rows
    target_loss = lax.dynamic_slice_in_dim(loss[0], at, rows, 0)
    far_grad = over(grad_send, 1)
    far_late = lax.optimization_barrier((far_late, grad_send))[0]
    pxt, ph1t, ph2, ps1, ps2 = whole(
        peer_kernel,
        kept,
        [x_type] + work,
        peer_near,
        peer_late,
        far_near,
        far_late,
        w_first,
        w_second,
        flops=2000000000,
    )

    step = ROW << (len(bits) - 1)
    stack = -(-(depth + hidden + classes) // step) * step

    def halves(n):
        return [((n // 2, LANE), BF), ((n // 2, LANE), F32)]

    send, keep = whole(
        functools.partial(back_kernel, bits[0]),
        halves(stack),
        [((stack, LANE), F32), ((2, node_dev, hidden), BF)],
        grad, far_grad, high, low, far_high, far_low,
        xt, pxt, h1t, ph1t, h2, ph2, s1, ps1, s2, ps2, w3t, w_second,
        limit=big,
    )
    size = stack // 2
    for at, bit in enumerate(bits[1:-1]):
        send, keep = whole(
            functools.partial(add_kernel, bit),
            halves(size),
            [((size, LANE), F32)],
            keep,
            over(send, bits[at]),
        )
        size //= 2
    for mine, bit in ((keep, bits[-2]), (None, bits[-1])):
        got = over(send, bit)
        (send,) = whole(sum_kernel, [((size, LANE), BF)], [], send if mine is None else mine, got)
    out = send
    for bit in reversed(bits[1:-1]):
        size *= 2
        (out,) = whole(functools.partial(join_kernel, bit), [((size, LANE), BF)], [], out, over(out, bit))
    pair = (out, over(out, bits[0]))
    across = [over(p, 1) for p in pair]
    cores = [other_core(p) for p in pair]
    both = [other_core(p) for p in across]
    first, second, third = whole(
        functools.partial(place_kernel, bits[0]),
        [((depth, hidden), BF), ((hidden, hidden), BF), ((classes, hidden), BF)],
        [],
        *pair,
        *across,
        *cores,
        *both,
    )
    return first, second, third.T, target_loss


def solution(mesh):
    in_specs = (
        P("owner", None),
        P(),
        P(),
        P(),
        P(("groups", "owner", "batch"), None),
        P(("groups", "owner", "batch"), None),
        P(("groups", "owner", "batch")),
    )
    out_specs = (
        P("groups", None),
        P("groups", None),
        P("groups", None),
        P(("groups", "owner", "batch")),
    )
    return jax.shard_map(body, mesh=mesh, in_specs=in_specs, out_specs=out_specs, check_vma=False)
```

```python
import functools
import jax
import jax.numpy as jnp
from jax import lax
from jax.experimental import pallas as pl
from jax.experimental.pallas import tpu as pltpu
from jax.sharding import PartitionSpec as P

BF = jnp.bfloat16
F32 = jnp.float32
ROW = 16
LANE = 128
PACK = 16


def nn(a, b):
    return lax.dot_general(a, b, (((1,), (0,)), ((), ())), preferred_element_type=F32)


def nt(a, b):
    return lax.dot_general(a, b, (((1,), (1,)), ((), ())), preferred_element_type=F32)


def tn(a, b):
    return lax.dot_general(a, b, (((0,), (0,)), ((), ())), preferred_element_type=F32)


def split(v):
    high = v.astype(BF)
    return high, (v - high.astype(F32)).astype(BF)


def device_slice():
    place = lax.rem(lax.axis_index("owner"), 2) * 2 + lax.axis_index("batch")
    return pl.multiple_of(place * LANE, LANE)


def activate(pre):
    sigma = 0.5 * jnp.tanh(0.5 * pre) + 0.5
    return (pre * sigma).astype(BF), sigma * (1.0 + pre * (1.0 - sigma))


def launch(sem, pairs):
    copies = [pltpu.make_async_copy(a, b, sem.at[i]) for i, (a, b) in enumerate(pairs)]
    for c in copies:
        c.start()
    return copies


def pack_kernel(nodes, ids_hbm, wts_hbm, labels_hbm, x_hbm, out, near, late, ids, wts, labels, sem):
    rows, fanout = ids.shape
    start = lax.axis_index("batch") * (x_hbm.shape[0] // 2)
    pairs = ((labels_hbm, labels), (ids_hbm, ids), (wts_hbm, wts))
    for piece in (near, late):
        pairs += ((x_hbm.at[pl.ds(pl.multiple_of(start, ROW), piece.shape[0]), :], piece),)
        start = start + piece.shape[0]
    into = launch(sem, pairs)
    for c in into[:3]:
        c.wait()
    shape = (rows, rows)
    same = lax.broadcasted_iota(jnp.int32, shape, 0) == lax.broadcasted_iota(jnp.int32, shape, 1)
    label = jnp.sum(jnp.where(same, labels[...].astype(F32), 0.0), axis=1, keepdims=True)
    out[:, :fanout] = ids[...].astype(F32) + label * nodes
    out[:, fanout:] = wts[...]
    into[3].wait()
    into[4].wait()


def load_kernel(after, *refs):
    del after
    count = len(refs) // 2
    for c in launch(refs[-1], tuple(zip(refs[:count], refs[count:-1]))):
        c.wait()


def own_kernel(x, w1, w2, w3, after, scores):
    del after
    hidden = activate(nn(x[...], w1[...]))[0]
    hidden = activate(nn(hidden, w2[...]))[0]
    scores[...] = nt(w3[...], hidden).astype(BF)


def layers(x, w1, w2, xt, h1t, h2, s1, s2, one, two):
    cols = pl.ds(device_slice(), LANE)
    rows = x[...]
    xt[...] = rows.T
    hidden, slope = activate(nn(rows, w1[...]))
    h1t[...] = hidden.T
    one[...] = slope
    s1[...] = one[:, cols]
    hidden, slope = activate(nn(hidden, w2[...]))
    two[...] = hidden
    s2[...] = slope
    h2[...] = two[:, cols]


def again_kernel(x, w1, w2, after, xt, h1t, h2, s1, s2, one, two):
    del after
    layers(x, w1, w2, xt, h1t, h2, s1, s2, one, two)


def peer_kernel(near, late, far_near, far_late, w1, w2, xt, h1t, h2, s1, s2, x, one, two):
    core = lax.axis_index("batch")
    for side, pieces in ((core, (near, late)), (1 - core, (far_near, far_late))):
        start = side * (x.shape[0] // 2)
        for piece in pieces:
            x[pl.ds(pl.multiple_of(start, ROW), piece.shape[0]), :] = piece[...]
            start = start + piece.shape[0]
    layers(x, w1, w2, xt, h1t, h2, s1, s2, one, two)


def spread(nodes, packed, high, low, label, ids, wts):
    fanout = ids.shape[0]
    targets = ids.shape[1]
    rows = packed.shape[0]
    node_dev = high.shape[0] // 2
    p = packed[...]
    if rows < LANE:
        p = jnp.concatenate([p] * (LANE // rows), axis=0)
    t = p.T
    parts = [t[i * fanout : (i + 1) * fanout] for i in range(4)]
    if rows < LANE:
        lane = lax.broadcasted_iota(jnp.int32, (fanout, LANE), 1)
        coded = jnp.where(lane < rows, parts[0], parts[2])
        wts[...] = jnp.where(lane < rows, parts[1], parts[3])
    else:
        coded = jnp.concatenate([parts[0], parts[2]], axis=1)
        wts[...] = jnp.concatenate([parts[1], parts[3]], axis=1)
    cls = jnp.floor(coded * (1.0 / nodes))
    label[...] = cls[0:1].astype(jnp.int32)
    ids[...] = (coded - cls * nodes).astype(jnp.int32)
    me = lax.axis_index("owner")
    block = 128
    per_side = node_dev // block

    def step(i, carry):
        side = i // per_side
        owner = jnp.where(side == 0, me, me + 1 - 2 * lax.rem(me, 2))
        base = owner * node_dev + lax.rem(i, per_side) * block
        node = lax.broadcasted_iota(jnp.int32, (block, LANE), 0) + base
        at = pl.ds(pl.multiple_of(i * block, block), block)
        for c in range(targets // LANE):
            cols = slice(c * LANE, (c + 1) * LANE)
            total = jnp.zeros((block, LANE), F32)
            for k in range(fanout):
                total += jnp.where(ids[k : k + 1, cols] == node, wts[k : k + 1, cols], 0.0)
            top, rest = split(total)
            high[at, cols] = top
            low[at, cols] = rest
        return carry

    lax.fori_loop(0, 2 * per_side, step, 0)


def logit_kernel(mine, theirs, high, low, part, send):
    n = mine.shape[1]
    total = nn(mine[...], high[:n]) + nn(mine[...], low[:n])
    total += nn(theirs[...], high[n:]) + nn(theirs[...], low[n:])
    part[...] = total
    send[...] = total.astype(BF)


def spread_kernel(nodes, packed, high, low, label, ids, wts):
    spread(nodes, packed, high, low, label, ids, wts)


def softmax_kernel(logits, got, label, grad, send, loss):
    v = logits[...] + got[...].astype(F32)
    top = jnp.max(v, axis=0, keepdims=True)
    e = jnp.exp(v - top)
    total = jnp.sum(e, axis=0, keepdims=True)
    hit = lax.broadcasted_iota(jnp.int32, v.shape, 0) == label[...]
    loss[...] = jnp.log(total) + top - jnp.sum(jnp.where(hit, v, 0.0), axis=0, keepdims=True)
    g = e / total - jnp.where(hit, 1.0, 0.0)
    grad[...] = g
    send[...] = g.astype(BF)


def back_kernel(bit, grad, far_grad, high, low, far_high, far_low, xt, pxt, h1t, ph1t, h2, ph2, s1, ps1, s2, ps2, w3t, w2, send, keep, acc, two):
    top, rest = split(grad[...])
    far = far_grad[...]
    depth, n = xt.shape
    hidden = h1t.shape[0]
    classes = w3t.shape[0]
    cols = pl.ds(device_slice(), LANE)
    w2_rows = w2[cols, :]
    sides = (slice(0, n), slice(n, 2 * n))
    own = jnp.concatenate([top, top], axis=1)
    other = jnp.concatenate([rest, far], axis=1)
    g = []
    for at in sides:
        total = nt(jnp.concatenate([high[at], low[at]], axis=1), own)
        total += nt(jnp.concatenate([high[at], far_high[at]], axis=1), other)
        g.append((total + nt(far_low[at], far)).astype(BF))
    b2 = [(nn(v, w3t[...]) * s[...]).astype(BF) for v, s in zip(g, (s2, ps2))]
    two[0] = b2[0]
    two[1] = b2[1]
    b1 = [(nt(v, w2_rows) * s[...]).astype(BF) for v, s in zip(b2, (s1, ps1))]
    acc[depth + hidden : depth + hidden + classes] = tn(g[0], h2[...]) + tn(g[1], ph2[...])
    acc[depth : depth + hidden] = nn(h1t[...], two[0, :, cols]) + nn(ph1t[...], two[1, :, cols])
    acc[:depth] = nn(xt[...], b1[0]) + nn(pxt[...], b1[1])
    blank = acc.shape[0] - (depth + hidden + classes)
    if blank:
        acc[depth + hidden + classes :] = jnp.zeros((blank, LANE), F32)
    halve(bit, acc, send, keep)


def halve(bit, acc, send, keep):
    rows = acc.shape[0] // 2
    up = lax.rem(lax.axis_index("owner") // bit, 2)
    send[...] = acc[pl.ds(pl.multiple_of((1 - up) * rows, 8), rows), :].astype(BF)
    keep[...] = acc[pl.ds(pl.multiple_of(up * rows, 8), rows), :]


def add_kernel(bit, kept, got, send, keep, acc):
    acc[...] = kept[...] + got[...].astype(F32)
    halve(bit, acc, send, keep)


def sum_kernel(kept, got, out):
    out[...] = (kept[...].astype(F32) + got[...].astype(F32)).astype(BF)


def join_kernel(bit, mine, got, out):
    rows = mine.shape[0]
    up = lax.rem(lax.axis_index("owner") // bit, 2)
    out[pl.ds(pl.multiple_of(up * rows, ROW), rows), :] = mine[...]
    out[pl.ds(pl.multiple_of((1 - up) * rows, ROW), rows), :] = got[...]


def fill(order, halves, sides, outs):
    rows = halves[0].shape[0]
    for i, (s, h) in enumerate(sides):
        cols = pl.ds(pl.multiple_of((2 * s + h) * LANE, LANE), LANE)
        for j in range(2):
            ref = halves[2 * i + order[j]]
            if ref is None:
                continue
            top = 0
            for out in outs:
                low, high = max(top, j * rows), min(top + out.shape[0], (j + 1) * rows)
                if low < high:
                    out[low - top : high - top, cols] = ref[low - j * rows : high - j * rows]
                top += out.shape[0]


def place_kernel(bit, *refs):
    halves, outs = refs[:8], refs[8:]
    me = lax.axis_index("owner")
    side = lax.rem(me, 2)
    core = lax.axis_index("batch")
    up = lax.rem(me // bit, 2)
    sides = ((side, core), (1 - side, core), (side, 1 - core), (1 - side, 1 - core))

    @pl.when(up == 0)
    def _():
        fill((0, 1), halves, sides, outs)

    @pl.when(up == 1)
    def _():
        fill((1, 0), halves, sides, outs)


def whole(kernel, outs, scratch, *args, flops=1000000, limit=24, far_in=(), far_out=()):
    def spec(i, far):
        return pl.BlockSpec(memory_space=pltpu.HBM if i in far else pltpu.VMEM)

    args = [
        pltpu.with_memory_space_constraint(x, pltpu.HBM) if i in far_in else x for i, x in enumerate(args)
    ]
    return pl.pallas_call(
        kernel,
        out_shape=[jax.ShapeDtypeStruct(shape, kind) for shape, kind in outs],
        in_specs=[spec(i, far_in) for i in range(len(args))],
        out_specs=[spec(i, far_out) for i in range(len(outs))],
        scratch_shapes=[
            pltpu.SemaphoreType.DMA((s,)) if isinstance(s, int) else pltpu.VMEM(*s) for s in scratch
        ],
        compiler_params=pltpu.CompilerParams(vmem_limit_bytes=limit << 20),
        cost_estimate=pl.CostEstimate(flops=flops, bytes_accessed=flops // 512, transcendentals=0),
    )(*args)


def body(features, w_first, w_second, w_third, nbr_ids, nbr_weight, labels):
    owners = lax.axis_size("owner")
    node_dev, depth = features.shape
    hidden, classes = w_third.shape
    rows, fanout = nbr_ids.shape
    nodes = owners * node_dev
    me = lax.axis_index("owner")
    core = lax.axis_index("batch")
    bits = [1 << i for i in range(1, owners.bit_length() - 1)]
    targets = owners * rows

    def over(x, bit):
        return lax.ppermute(x, "owner", [(i, i ^ bit) for i in range(owners)])

    def other_core(x):
        return lax.ppermute(x, "batch", [(0, 1), (1, 0)])

    w3t = w_third.T
    near = 5 * node_dev // 16
    w1_type, w2_type, x_type = (w_first.shape, BF), (w_second.shape, BF), (features.shape, BF)
    packed, my_near, my_late = whole(
        functools.partial(pack_kernel, nodes),
        [((rows, 2 * fanout), F32), ((near, depth), BF), ((node_dev // 2 - near, depth), BF)],
        [((rows, fanout), jnp.int32), ((rows, fanout), F32), ((1, rows), jnp.int32), 5],
        nbr_ids,
        nbr_weight,
        labels.reshape(1, rows),
        features,
        limit=PACK,
        far_in=range(4),
    )
    peer_near = over(my_near, 1)
    got = other_core(packed)
    packed = jnp.where(core == 0, jnp.concatenate([packed, got], 1), jnp.concatenate([got, packed], 1))
    features, w_first, w_second, w3t = whole(
        load_kernel,
        [x_type, w1_type, w2_type, (w3t.shape, BF)],
        [4],
        packed,
        features,
        w_first,
        w_second,
        w3t,
        limit=PACK,
        far_in=range(1, 5),
    )
    (scores,) = whole(
        own_kernel,
        [((classes, node_dev), BF)],
        [],
        features,
        w_first,
        w_second,
        w3t,
        packed,
        flops=1000,
        limit=16,
    )
    for bit in bits:
        got = over(packed, bit)
        if bit == bits[0]:
            got, scores = lax.optimization_barrier((got, scores))
        if bit == bits[-1]:
            got, peer_near = lax.optimization_barrier((got, peer_near))
        up = (me // bit) % 2
        packed = jnp.where(up == 0, jnp.concatenate([packed, got], 0), jnp.concatenate([got, packed], 0))
    far_scores = over(scores, 1)

    big = 24 if owners <= 8 else 48
    maps = [((2 * node_dev, targets), BF), ((2 * node_dev, targets), BF), ((1, targets), jnp.int32)]
    tables = [((fanout, targets), jnp.int32), ((fanout, targets), F32)]
    spread_call = functools.partial(whole, functools.partial(spread_kernel, nodes), maps, tables, limit=big, flops=1000000000)
    high, low, label = spread_call(packed)
    my_late = lax.optimization_barrier((my_late, high))[0]
    peer_late = over(my_late, 1)
    part, send = whole(
        logit_kernel,
        [((classes, targets), F32), ((classes, targets), BF)],
        [],
        scores,
        far_scores,
        high,
        low,
        limit=big,
    )
    kept = [
        ((depth, node_dev), BF),
        ((hidden, node_dev), BF),
        ((node_dev, LANE), BF),
        ((node_dev, LANE), F32),
        ((node_dev, hidden), F32),
    ]
    work = [((node_dev, hidden), F32), ((node_dev, hidden), BF)]
    packed = lax.optimization_barrier((packed, send))[0]
    far_packed = over(packed, 1)
    xt, h1t, h2, s1, s2 = whole(
        again_kernel, kept, work, features, w_first, w_second, send, flops=1000
    )
    peer_near, peer_late = lax.optimization_barrier((peer_near, peer_late, s1))[:2]
    far_near, far_late = other_core(peer_near), other_core(peer_late)
    for bit in bits[:-1]:
        got = over(send, bit)
        if bit == bits[0]:
            got = lax.optimization_barrier((got, s1))[0]
        part = part + got.astype(F32)
        send = part.astype(BF)
    far_packed = lax.optimization_barrier((far_packed, send))[0]
    far_high, far_low, _ = spread_call(far_packed)
    got = over(send, bits[-1])
    got = lax.optimization_barrier((got, far_high))[0]
    grad, grad_send, loss = whole(
        softmax_kernel,
        [((classes, targets), F32), ((classes, targets), BF), ((1, targets), F32)],
        [],
        part,
        got,
        label,
    )
    at = core * (targets // 2) + (me // 2) * rows
    target_loss = lax.dynamic_slice_in_dim(loss[0], at, rows, 0)
    far_grad = over(grad_send, 1)
    far_late = lax.optimization_barrier((far_late, grad_send))[0]
    pxt, ph1t, ph2, ps1, ps2 = whole(
        peer_kernel,
        kept,
        [x_type] + work,
        peer_near,
        peer_late,
        far_near,
        far_late,
        w_first,
        w_second,
        flops=2000000000,
    )

    step = ROW << (len(bits) - 1)
    stack = -(-(depth + hidden + classes) // step) * step

    def halves(n):
        return [((n // 2, LANE), BF), ((n // 2, LANE), F32)]

    send, keep = whole(
        functools.partial(back_kernel, bits[0]),
        halves(stack),
        [((stack, LANE), F32), ((2, node_dev, hidden), BF)],
        grad, far_grad, high, low, far_high, far_low,
        xt, pxt, h1t, ph1t, h2, ph2, s1, ps1, s2, ps2, w3t, w_second,
        limit=big,
    )
    size = stack // 2
    for at, bit in enumerate(bits[1:-1]):
        send, keep = whole(
            functools.partial(add_kernel, bit),
            halves(size),
            [((size, LANE), F32)],
            keep,
            over(send, bits[at]),
        )
        size //= 2
    for mine, bit in ((keep, bits[-2]), (None, bits[-1])):
        got = over(send, bit)
        (send,) = whole(sum_kernel, [((size, LANE), BF)], [], send if mine is None else mine, got)
    out = send
    for bit in reversed(bits[1:-1]):
        size *= 2
        (out,) = whole(functools.partial(join_kernel, bit), [((size, LANE), BF)], [], out, over(out, bit))
    pair = (out, over(out, bits[0]))
    across = [over(p, 1) for p in pair]
    cores = [other_core(p) for p in pair]
    both = [other_core(p) for p in across]
    first, second, third = whole(
        functools.partial(place_kernel, bits[0]),
        [((depth, hidden), BF), ((hidden, hidden), BF), ((classes, hidden), BF)],
        [],
        *pair,
        *across,
        *cores,
        *both,
    )
    return first, second, third.T, target_loss


def solution(mesh):
    in_specs = (
        P("owner", None),
        P(),
        P(),
        P(),
        P(("groups", "owner", "batch"), None),
        P(("groups", "owner", "batch"), None),
        P(("groups", "owner", "batch")),
    )
    out_specs = (
        P("groups", None),
        P("groups", None),
        P("groups", None),
        P(("groups", "owner", "batch")),
    )
    return jax.shard_map(body, mesh=mesh, in_specs=in_specs, out_specs=out_specs, check_vma=False)
```
